128 devices in a mesh: node: 16 (over x, z), local: 8 (over y, core).
Axes of the slice: x: 4, y: 4, z: 4, core: 2. Of those that a mesh axis runs over, the one named last changes fastest.
Arguments:
- owner_map: int32 [128], replicated, may hold values from 0 to 127, as said below
- bag_sizes: int32 [128, 8192], P(('node', 'local')), may hold values from 1 to 8
- indices: int32 [128, 8192, 8], P(('node', 'local')), may hold values from 0 to 2047
- tables: bfloat16 [262144, 128], P(('node', 'local')), may hold values from -2 to 2
- cross_down: bfloat16 [128, 128, 512], P('local'), may hold values from -0.046875 to 0.046875
- cross_up: bfloat16 [512, 128, 128], P(None, 'local'), may hold values from -0.25 to 0.25
- cross_bias: float32 [128, 128], P('local'), may hold values from -3 to 3
- mlp_weight: bfloat16 [128, 128, 2048], P('local'), may hold values from -0.046875 to 0.046875
- mlp_bias: float32 [2048], replicated, may hold values from -3 to 3
- hidden_grad: bfloat16 [8192, 2048], P('node'), may hold values from -6 to 6
Outputs:
- crossed: bfloat16 [128, 8192, 128], P('local', 'node')
- hidden: bfloat16 [8192, 2048], P('node', 'local')
- table_grad: float32 [262144, 128], P(('node', 'local'))
The draws below stay inside these ranges and needn't reach their ends.
Inputs may be any that keep to these rules, and one draw needn't show every extreme that they name: owner_map is a permutation of the devices: each device owns exactly one feature. Call f // 16 the group of feature f; the devices with one local index own at most 3 features of one group, and exactly 3 for some local index and group in every draw.
All inputs are finite; a program needn't handle non-finite values.
Results may differ from the reference program's by a relative error of at most 0.015.
Values may be sent and summed in bfloat16 or wider, within the bound.
A program may use at most 128 MiB of HBM per device.

```python
import jax
import jax.numpy as jnp
from jax import lax

EMB = 128
RANK = 512
HIDDEN_SIZE = 2048
BAG = 8
ROWS_TAB = 2048
SAMP_NODE = 512
FEATURES = 128
B_TOTAL = 8192
N_NODE = 16
N_LOCAL = 8
DEVICES = 128


def draw_owner_map(key, part):
    key = jax.random.fold_in(key, 7)
    keys = jax.random.split(key, 6)
    lanes = N_LOCAL
    base_count = N_NODE // N_LOCAL
    row_first = jax.random.randint(keys[0], (), 0, lanes)
    row_second = (row_first + jax.random.randint(keys[1], (), 1, lanes)) % lanes
    col_first = jax.random.randint(keys[2], (), 0, lanes)
    col_second = (col_first + jax.random.randint(keys[3], (), 1, lanes)) % lanes
    counts = jnp.full((lanes, lanes), base_count, jnp.int32)
    counts = counts.at[row_first, col_first].add(1).at[row_second, col_second].add(1)
    counts = counts.at[row_first, col_second].add(-1).at[row_second, col_first].add(-1)
    upto = jnp.cumsum(counts, axis=0).astype(jnp.int32)
    slot_ids = jnp.arange(N_NODE, dtype=jnp.int32)
    upto_by_group = upto.T
    column = jnp.sum((slot_ids[None, :, None] >= upto_by_group[:, None, :]).astype(jnp.int32), axis=2).astype(jnp.int32)
    starts = (upto - counts).T
    start_here = jnp.take_along_axis(starts, column, axis=1)
    before = (jnp.cumsum(counts, axis=1) - counts).astype(jnp.int32).T
    before_here = jnp.take_along_axis(before, column, axis=1)
    rank_in_lane = (before_here + slot_ids[None, :] - start_here).astype(jnp.int32)
    node_perms = jax.vmap(lambda k: jax.random.permutation(k, N_NODE))(jax.random.split(keys[4], lanes)).astype(jnp.int32)
    node_pick = node_perms[column, rank_in_lane]
    owners = node_pick * lanes + column
    feat_perms = jax.vmap(lambda k: jax.random.permutation(k, N_NODE))(jax.random.split(keys[5], lanes)).astype(jnp.int32)
    feature = jnp.arange(lanes, dtype=jnp.int32)[:, None] * N_NODE + feat_perms
    result = jnp.zeros((N_NODE * N_LOCAL,), jnp.int32).at[feature.reshape(-1)].set(owners.reshape(-1).astype(jnp.int32))
    return result


def plant(array, stream_key, least, largest):
    index_at = [jax.random.randint(jax.random.fold_in(stream_key, axis), (), 0, length) for axis, length in enumerate(array.shape)]
    main_axis = array.shape.index(max(array.shape))
    next_to = index_at[:main_axis] + [(index_at[main_axis] + 1) % array.shape[main_axis]] + index_at[main_axis + 1:]
    return array.at[tuple(index_at)].set(least).at[tuple(next_to)].set(largest)


def block_levels(own_key, extent, cuts, smallest, largest):
    gain, own = 1.0, jax.random.fold_in(own_key, 6)
    for position, parts in cuts:
        steps = jnp.exp(jax.random.uniform(jax.random.fold_in(own, position), (parts,), jnp.float32, smallest / len(cuts), largest / len(cuts)))
        gain = gain * jnp.repeat(steps, extent[position] // parts).reshape([-1 if axis == position else 1 for axis in range(len(extent))])
    return gain


def normal_values(stream_key, shape, scale, bound, pieces=(), kind=jnp.bfloat16):
    level = block_levels(stream_key, shape, pieces, -0.22, 0.18) if pieces else 1.0
    drawn = jax.random.normal(stream_key, shape, jnp.float32) * scale * level
    return jnp.minimum(jnp.maximum(drawn, -bound), bound).astype(kind)


def setup_inputs(seed: int = 0) -> dict:
    splits = jax.random.split(jax.random.key(seed), 11)
    return {
        "owner_map": draw_owner_map(jax.random.fold_in(splits[10], 71), 0),
        "bag_sizes": plant(jax.random.randint(splits[1], (DEVICES, B_TOTAL), 1, BAG + 1), jax.random.fold_in(splits[1], 1), 1, BAG).astype(jnp.int32),
        "indices": plant(jax.random.randint(splits[2], (DEVICES, B_TOTAL, BAG), 0, ROWS_TAB), jax.random.fold_in(splits[2], 1), 0, ROWS_TAB - 1).astype(jnp.int32),
        "tables": normal_values(splits[3], (DEVICES * ROWS_TAB, EMB), 0.35, 2.0, ((0, 128),)),
        "cross_down": normal_values(splits[4], (FEATURES, EMB, RANK), (FEATURES * EMB) ** -0.5, 0.046875, ((0, 8),)),
        "cross_up": normal_values(splits[5], (RANK, FEATURES, EMB), RANK ** -0.5, 0.25, ((1, 8),)),
        "cross_bias": normal_values(splits[6], (FEATURES, EMB), 0.5, 3.0, ((0, 8),), jnp.float32),
        "mlp_weight": normal_values(splits[7], (FEATURES, EMB, HIDDEN_SIZE), (FEATURES * EMB) ** -0.5, 0.046875, ((0, 8),)),
        "mlp_bias": normal_values(splits[8], (HIDDEN_SIZE,), 0.5, 3.0, (), jnp.float32),
        "hidden_grad": normal_values(splits[9], (B_TOTAL, HIDDEN_SIZE), 1.0, 6.0, ((0, 16),)),
    }


def reference(owner_map, bag_sizes, indices, tables, cross_down, cross_up, cross_bias, mlp_weight, mlp_bias, hidden_grad):
    devices = owner_map.shape[0]
    emb_width = tables.shape[1]
    rows_tab = tables.shape[0] // devices
    bag_depth = indices.shape[2]
    batch_total = indices.shape[1]
    table_blocks = tables.reshape(devices, rows_tab, emb_width)

    def pool_one(inputs):
        table_block, row_picks, bag_counts = inputs
        looked_up = jnp.take(table_block, row_picks, axis=0).astype(jnp.float32)
        in_bag = (jnp.arange(bag_depth, dtype=jnp.int32)[None, :] < bag_counts[:, None]).astype(jnp.float32)
        return jnp.einsum('bj,bje->be', in_bag, looked_up).astype(jnp.bfloat16)

    pooled = lax.map(pool_one, (table_blocks, indices, bag_sizes))
    x_zero = jnp.take(pooled, owner_map, axis=0)
    block_count = batch_total // SAMP_NODE
    x_blocks = x_zero.reshape(devices, block_count, SAMP_NODE, emb_width).transpose(1, 0, 2, 3)
    grad_blocks = hidden_grad.reshape(block_count, SAMP_NODE, hidden_grad.shape[1])
    down_float = cross_down.astype(jnp.float32)
    up_float = cross_up.astype(jnp.float32)
    weight_float = mlp_weight.astype(jnp.float32)

    def layer(inputs):
        inputs_now, grad_out = inputs
        x_float = inputs_now.astype(jnp.float32)
        low_rank = jnp.einsum('qse,qer->sr', x_float, down_float).astype(jnp.bfloat16)
        cross_term = jnp.einsum('sr,rqe->qse', low_rank.astype(jnp.float32), up_float) + cross_bias[:, None, :]
        crossed = (x_float * cross_term + x_float).astype(jnp.bfloat16)
        pre_act = jnp.einsum('qse,qeh->sh', crossed.astype(jnp.float32), weight_float) + mlp_bias
        hidden = jax.nn.silu(pre_act).astype(jnp.bfloat16)
        sig_pre = jax.nn.sigmoid(pre_act)
        grad_pre = (grad_out.astype(jnp.float32) * sig_pre * (1.0 + pre_act * (1.0 - sig_pre))).astype(jnp.bfloat16)
        grad_crossed = jnp.einsum('sh,qeh->qse', grad_pre.astype(jnp.float32), weight_float)
        grad_cross = (grad_crossed * x_float).astype(jnp.bfloat16)
        grad_rank = jnp.einsum('qse,rqe->sr', grad_cross.astype(jnp.float32), up_float).astype(jnp.bfloat16)
        grad_input = grad_crossed * cross_term + grad_crossed + jnp.einsum('sr,qer->qse', grad_rank.astype(jnp.float32), down_float)
        return crossed, hidden, grad_input.astype(jnp.bfloat16)

    crossed_blocks, hidden_blocks, grad_input_blocks = lax.map(layer, (x_blocks, grad_blocks))
    crossed = crossed_blocks.transpose(1, 0, 2, 3).reshape(devices, batch_total, emb_width)
    hidden = hidden_blocks.reshape(batch_total, hidden_grad.shape[1])
    grad_x_zero = grad_input_blocks.transpose(1, 0, 2, 3).reshape(devices, batch_total, emb_width)
    grad_by_owner = jnp.zeros_like(grad_x_zero).at[owner_map].set(grad_x_zero)

    def accumulate(inputs):
        row_picks, bag_counts, grad_rows = inputs
        in_bag = (jnp.arange(bag_depth, dtype=jnp.int32)[None, :] < bag_counts[:, None]).astype(jnp.float32)
        terms = grad_rows.astype(jnp.float32)[:, None, :] * in_bag[:, :, None]
        empty = jnp.zeros((rows_tab, emb_width), jnp.float32)
        return empty.at[row_picks.reshape(-1)].add(terms.reshape(-1, emb_width))

    table_grad = lax.map(accumulate, (indices, bag_sizes, grad_by_owner)).reshape(devices * rows_tab, emb_width)
    return crossed, hidden, table_grad
```

```python
import functools

import jax
import jax.numpy as jnp
from jax import lax
from jax.experimental import pallas as pl
from jax.experimental.pallas import tpu as pltpu
from jax.sharding import PartitionSpec as P

BF = jnp.bfloat16
F32 = jnp.float32
MESH = pl.DeviceIdType.MESH
PIECES = 4
BAG_GROUP = 32
LOW = 256


def dot(a, b, contract=((1,), (0,))):
    return lax.dot_general(a, b, (contract, ((), ())), preferred_element_type=F32)


def greet(n_node, n_local, node, lane):
    barrier = pltpu.get_barrier_semaphore()

    def by_node(k, carry):
        peer = lax.rem(node + k, n_node)
        pl.semaphore_signal(barrier, inc=1, device_id=(peer, lane), device_id_type=MESH)
        return carry

    def by_lane(d, carry):
        peer = lax.rem(lane + d, n_local)
        pl.semaphore_signal(barrier, inc=1, device_id=(node, peer), device_id_type=MESH)
        return carry

    lax.fori_loop(1, n_node, by_node, 0)
    lax.fori_loop(1, n_local, by_lane, 0)
    pl.semaphore_wait(barrier, n_node + n_local - 2)


def flatten_picks(idx_ref, size_ref, iota_ref, key_ref, low_ref):
    iota_ref[...] = lax.broadcasted_iota(jnp.int32, iota_ref.shape, 0).astype(F32).astype(BF)
    lanes = lax.broadcasted_iota(jnp.int32, (1, 128), 1)
    depth = lax.broadcasted_iota(jnp.int32, (8, 128), 0)

    def eight_groups(b, carry):
        rows = [[], []]
        for half in range(2):
            off = pl.multiple_of(b * 256 + half * 128, 128)
            picks = jnp.where(depth < size_ref[:, pl.ds(off, 128)], idx_ref[:, pl.ds(off, 128)], -1)
            turned = [picks] + [pltpu.roll(picks, 32 * d, 1) for d in (1, 2, 3)]
            for group in range(4):
                for h in range(2):
                    row = turned[(3 - group) % 4][4 * h + 3 : 4 * h + 4]
                    for q in (2, 1, 0):
                        source = turned[(q - group) % 4][4 * h + q : 4 * h + q + 1]
                        row = jnp.where(lanes < 32 * (q + 1), source, row)
                    rows[h].append(row)
        here = pl.ds(pl.multiple_of(b * 8, 8), 8)
        for h in range(2):
            picks = jnp.concatenate(rows[h], 0)
            key_ref[here, h * 128 : (h + 1) * 128] = ((picks >> 8) * 32 + (lanes & 31)).astype(F32)
            low_ref[here, h * 128 : (h + 1) * 128] = (picks & 255).astype(F32)
        return carry

    lax.fori_loop(0, idx_ref.shape[1] // 256, eight_groups, 0)


def count_group(key_ref, low_ref, iota_ref, group):
    iota = iota_ref[...]
    one, zero = jnp.ones((), BF), jnp.zeros((), BF)
    hot = []
    for ref in (key_ref, low_ref):
        row = jnp.broadcast_to(ref[pl.ds(group, 1), :], (16, LOW)).astype(BF)
        hot.append(jnp.where(jnp.concatenate([row] * 16, 0) == iota, one, zero))
    return dot(hot[0], hot[1], ((1,), (1,))).astype(BF)


def put_counts(count_ref, where, row, counts):
    for h in range(8):
        columns = slice(h * LOW, (h + 1) * LOW)
        if where is None:
            count_ref[pl.ds(row, BAG_GROUP), columns] = counts[h * 32 : (h + 1) * 32]
        else:
            count_ref[where, pl.ds(row, BAG_GROUP), columns] = counts[h * 32 : (h + 1) * 32]


def pool_kernel(
    n_node, n_local, pick_ref, slot_ref, idx_ref, size_ref, table_ref, x_ref,
    iota, key, low, counts, pooled, packed, node_send, node_recv, lane_send, lane_recv, *places,
):
    node, lane = lax.axis_index("node"), lax.axis_index("local")
    arrived, landed = places[:PIECES], places[PIECES:]
    cap = packed.shape[2]
    rows = pooled.shape[2]
    per_node = PIECES * rows // BAG_GROUP
    greet(n_node, n_local, node, lane)
    flatten_picks(idx_ref, size_ref, iota, key, low)

    def to_node(p, k):
        return pltpu.make_async_remote_copy(
            src_ref=pooled.at[p, k],
            dst_ref=arrived[p].at[node],
            send_sem=node_send.at[p, k],
            recv_sem=node_recv.at[p, k],
            device_id=(lax.rem(node + k, n_node), lane),
            device_id_type=MESH,
        )

    def to_lane(p, d):
        return pltpu.make_async_remote_copy(
            src_ref=packed.at[p, d],
            dst_ref=landed[p].at[pl.ds(lane * cap, cap)],
            send_sem=lane_send.at[p, d],
            recv_sem=lane_recv.at[p, d],
            device_id=(node, lax.rem(lane + d, n_local)),
            device_id_type=MESH,
        )

    def pool_piece(p):
        def four_nodes(c, carry):
            for i in range(16):
                source = lax.rem(node + c * 4 + i // 4, n_node)
                group = source * per_node + p * 4 + i % 4
                put_counts(counts, None, i * BAG_GROUP, count_group(key, low, iota, group))
            sums = dot(counts[...], table_ref[...]).astype(BF)
            for i in range(4):
                pooled[p, c * 4 + i] = sums[i * rows : (i + 1) * rows]

            for piece in range(PIECES):

                @pl.when(p == piece)
                def _():
                    def send(k, inner):
                        to_node(piece, k).start()
                        return inner

                    lax.fori_loop(jnp.maximum(c * 4, 1), c * 4 + 4, send, 0)

            return carry

        lax.fori_loop(0, n_node // 4, four_nodes, 0)

    def pack_piece(p):
        def arrive(k, carry):
            to_node(p, k).wait_recv()
            return carry

        lax.fori_loop(1, n_node, arrive, 0)
        arrived[p][node] = pooled[p, 0]
        for c in range(cap):
            landed[p][lane * cap + c] = arrived[p][pick_ref[lane * cap + c]]

        def send(d, carry):
            target = lax.rem(lane + d, n_local)
            for c in range(cap):
                packed[p, d, c] = arrived[p][pick_ref[target * cap + c]]
            to_lane(p, d).start()
            return carry

        lax.fori_loop(1, n_local, send, 0)

    def unpack_piece(p):
        def land(d, carry):
            to_lane(p, d).wait_recv()
            return carry

        lax.fori_loop(1, n_local, land, 0)
        for q in range(n_node):
            x_ref[p * rows : (p + 1) * rows, q * 128 : (q + 1) * 128] = landed[p][slot_ref[q]]

    def turn(p, carry):
        pool_piece(p)
        for piece in range(PIECES - 1):

            @pl.when(p == piece + 1)
            def _():
                pack_piece(piece)

        return carry

    lax.fori_loop(0, PIECES, turn, 0)
    pack_piece(PIECES - 1)

    for p in range(PIECES):
        unpack_piece(p)

        def sent_node(k, inner):
            to_node(p, k).wait_send()
            return inner

        def sent_lane(d, inner):
            to_lane(p, d).wait_send()
            return inner

        lax.fori_loop(1, n_node, sent_node, 0)
        lax.fori_loop(1, n_local, sent_lane, 0)


def scatter_kernel(
    n_node, n_local, pick_ref, slot_ref, idx_ref, size_ref, grad_ref, out_ref,
    iota, key, low, counts, packed, routed, home, home_t, total, lane_send, lane_recv, node_send, node_recv, *landed,
):
    node, lane = lax.axis_index("node"), lax.axis_index("local")
    cap = packed.shape[2]
    rows = packed.shape[3]
    per_node = PIECES * rows // BAG_GROUP
    greet(n_node, n_local, node, lane)

    def to_lane(p, d):
        return pltpu.make_async_remote_copy(
            src_ref=packed.at[p, d],
            dst_ref=landed[p].at[pl.ds(lane * cap, cap)],
            send_sem=lane_send.at[p, d],
            recv_sem=lane_recv.at[p, d],
            device_id=(node, lax.rem(lane + d, n_local)),
            device_id_type=MESH,
        )

    def to_node(p, k):
        return pltpu.make_async_remote_copy(
            src_ref=routed.at[p, k],
            dst_ref=home.at[p, node],
            send_sem=node_send.at[p, k],
            recv_sem=node_recv.at[p, k],
            device_id=(lax.rem(node + k, n_node), lane),
            device_id_type=MESH,
        )

    def pack_piece(p):
        here = slice(p * rows, (p + 1) * rows)

        def send(d, inner):
            target = lax.rem(lane + d, n_local)
            for c in range(cap):
                packed[p, d, c] = grad_ref[pick_ref[target * cap + c], here]
            to_lane(p, d).start()
            return inner

        lax.fori_loop(1, n_local, send, 0)
        for c in range(cap):
            landed[p][lane * cap + c] = grad_ref[pick_ref[lane * cap + c], here]

    def count_piece(p):
        def four_nodes(c, carry):
            for i in range(16):
                group = (c * 4 + i // 4) * per_node + p * 4 + i % 4
                row = pl.multiple_of(c * 16 * BAG_GROUP + i * BAG_GROUP, BAG_GROUP)
                put_counts(counts, p, row, count_group(key, low, iota, group))
            return carry

        lax.fori_loop(0, n_node // 4, four_nodes, 0)

    def route_piece(p):
        def land(d, carry):
            to_lane(p, d).wait_recv()
            return carry

        lax.fori_loop(1, n_local, land, 0)

        def send(k, carry):
            routed[p, k] = landed[p][slot_ref[lax.rem(node + k, n_node)]]
            to_node(p, k).start()
            return carry

        lax.fori_loop(1, n_node, send, 0)
        home[p, node] = landed[p][slot_ref[node]]

    def add_piece(p):
        def arrive(k, carry):
            to_node(p, k).wait_recv()
            return carry

        lax.fori_loop(1, n_node, arrive, 0)
        for n in range(n_node):
            home_t[:, n * rows : (n + 1) * rows] = home[p, n].T

        def columns(c, carry):
            here = pl.ds(pl.multiple_of(c * 512, 512), 512)
            total[:, here] += dot(home_t[...], counts[p, :, here])
            return carry

        lax.fori_loop(0, total.shape[1] // 512, columns, 0)

    for p in range(PIECES):
        pack_piece(p)
    flatten_picks(idx_ref, size_ref, iota, key, low)
    total[...] = jnp.zeros_like(total)

    def turn(p, carry):
        @pl.when(p < PIECES)
        def _():
            count_piece(p)

        for piece in range(PIECES):

            @pl.when(p == piece + 2)
            def _():
                route_piece(piece)

        @pl.when(p >= 3)
        def _():
            add_piece(p - 3)

        return carry

    lax.fori_loop(0, PIECES + 3, turn, 0)
    for n in range(total.shape[1] // 128):
        out_ref[n * 128 : (n + 1) * 128, :] = total[:, n * 128 : (n + 1) * 128].T

    for p in range(PIECES):

        def sent_node(k, inner):
            to_node(p, k).wait_send()
            return inner

        def sent_lane(d, inner):
            to_lane(p, d).wait_send()
            return inner

        lax.fori_loop(1, n_node, sent_node, 0)
        lax.fori_loop(1, n_local, sent_lane, 0)


SMEM = pl.BlockSpec(memory_space=pltpu.SMEM)
VMEM = pl.BlockSpec(memory_space=pltpu.VMEM)
SEM = pltpu.SemaphoreType.DMA


def pool_and_send(pick, slot, picks, sizes, tables, n_node, n_local, cap, samples):
    rows = samples // PIECES
    groups = picks.shape[1] // BAG_GROUP
    width = tables.shape[1]
    return pl.pallas_call(
        functools.partial(pool_kernel, n_node, n_local),
        out_shape=jax.ShapeDtypeStruct((samples, n_node * width), BF),
        in_specs=[SMEM, SMEM, VMEM, VMEM, VMEM],
        out_specs=VMEM,
        scratch_shapes=[
            pltpu.VMEM((LOW, LOW), BF),
            pltpu.VMEM((groups, LOW), F32),
            pltpu.VMEM((groups, LOW), F32),
            pltpu.VMEM((16 * BAG_GROUP, tables.shape[0]), BF),
            pltpu.VMEM((PIECES, n_node, rows, width), BF),
            pltpu.VMEM((PIECES, n_local, cap, rows, width), BF),
            SEM((PIECES, n_node)),
            SEM((PIECES, n_node)),
            SEM((PIECES, n_local)),
            SEM((PIECES, n_local)),
            *[pltpu.VMEM((n_node, rows, width), BF)] * PIECES,
            *[pltpu.VMEM((n_local * cap, rows, width), BF)] * PIECES,
        ],
        compiler_params=pltpu.CompilerParams(collective_id=0, has_side_effects=True, vmem_limit_bytes=48 << 20),
        name="pool_and_send",
    )(pick, slot, picks, sizes, tables)


def send_and_scatter(pick, slot, picks, sizes, grads, table_rows, n_node, n_local, cap):
    samples, width = grads.shape[1:]
    rows = samples // PIECES
    groups = picks.shape[1] // BAG_GROUP
    return pl.pallas_call(
        functools.partial(scatter_kernel, n_node, n_local),
        out_shape=jax.ShapeDtypeStruct((table_rows, width), F32),
        in_specs=[SMEM, SMEM, VMEM, VMEM, VMEM],
        out_specs=VMEM,
        scratch_shapes=[
            pltpu.VMEM((LOW, LOW), BF),
            pltpu.VMEM((groups, LOW), F32),
            pltpu.VMEM((groups, LOW), F32),
            pltpu.VMEM((PIECES, n_node * rows, table_rows), BF),
            pltpu.VMEM((PIECES, n_local, cap, rows, width), BF),
            pltpu.VMEM((PIECES, n_node, rows, width), BF),
            pltpu.VMEM((PIECES, n_node, rows, width), BF),
            pltpu.VMEM((width, n_node * rows), BF),
            pltpu.VMEM((width, table_rows), F32),
            SEM((PIECES, n_local)),
            SEM((PIECES, n_local)),
            SEM((PIECES, n_node)),
            SEM((PIECES, n_node)),
            *[pltpu.VMEM((n_local * cap, rows, width), BF)] * PIECES,
        ],
        compiler_params=pltpu.CompilerParams(collective_id=1, has_side_effects=True, vmem_limit_bytes=56 << 20),
        name="send_and_scatter",
    )(pick, slot, picks, sizes, grads)


def on_device(
    owner_map,
    bag_sizes,
    indices,
    tables,
    cross_down,
    cross_up,
    cross_bias,
    mlp_weight,
    mlp_bias,
    hidden_grad,
):
    node_count = lax.axis_size("node")
    lane_count = lax.axis_size("local")
    my_lane = lax.axis_index("local")
    capacity = node_count // lane_count + 1
    slot_total = lane_count * capacity
    samples = hidden_grad.shape[0]
    emb_width = tables.shape[1]
    hidden_width = hidden_grad.shape[1]
    share_width = hidden_width // lane_count
    picks = indices[0].T
    feat_ids = jnp.arange(owner_map.shape[0], dtype=jnp.int32)
    node_ids = jnp.arange(node_count, dtype=jnp.int32)
    source_dev = node_ids * lane_count + my_lane
    source_feat = jnp.sum(
        jnp.where(owner_map[None, :] == source_dev[:, None], feat_ids[None, :], 0), axis=1
    )
    source_group = source_feat // node_count
    same_group = source_group[:, None] == source_group[None, :]
    earlier = node_ids[None, :] < node_ids[:, None]
    source_slot = source_group * capacity + jnp.sum(
        (same_group & earlier).astype(jnp.int32), axis=1
    )
    group_owners = lax.dynamic_slice_in_dim(owner_map, my_lane * node_count, node_count)
    owner_lane = group_owners % lane_count
    owner_node = group_owners // lane_count
    ahead_same = (owner_lane[:, None] == owner_lane[None, :]) & (
        owner_node[None, :] < owner_node[:, None]
    )
    owner_slot = owner_lane * capacity + jnp.sum(ahead_same.astype(jnp.int32), axis=1)
    slot_ids = jnp.arange(slot_total, dtype=jnp.int32)
    pick_source = jnp.sum(
        jnp.where(source_slot[None, :] == slot_ids[:, None], node_ids[None, :], 0), axis=1
    )
    back_source = jnp.sum(
        jnp.where(owner_slot[None, :] == slot_ids[:, None], node_ids[None, :], 0), axis=1
    )

    x_zero = pool_and_send(
        pick_source, owner_slot, picks, bag_sizes, tables, node_count, lane_count, capacity, samples
    )
    down = cross_down.reshape(-1, cross_down.shape[2])
    up = cross_up.reshape(cross_up.shape[0], -1)
    weight = mlp_weight.reshape(-1, hidden_width)
    partial_rank = dot(x_zero, down)
    low_rank = lax.psum(partial_rank, "local").astype(BF)
    cross_term = dot(low_rank, up) + cross_bias.reshape(1, -1)
    x_float = x_zero.astype(F32)
    crossed = (x_float * cross_term + x_float).astype(BF)
    partial_pre = dot(crossed, weight)
    share_start = my_lane * share_width
    pre_act = lax.psum(partial_pre, "local") + mlp_bias
    hidden = jax.nn.silu(lax.dynamic_slice_in_dim(pre_act, share_start, share_width, 1)).astype(BF)
    sig_pre = jax.nn.sigmoid(pre_act)
    grad_pre = (hidden_grad.astype(F32) * sig_pre * (1.0 + pre_act * (1.0 - sig_pre))).astype(BF)
    grad_crossed = dot(grad_pre, weight, ((1,), (1,)))
    grad_cross = (grad_crossed * x_float).astype(BF)
    partial_grad_rank = dot(grad_cross, up, ((1,), (1,)))
    grad_rank = lax.psum(partial_grad_rank.astype(BF), "local")
    grad_input = grad_crossed * cross_term + grad_crossed + dot(grad_rank, down, ((1,), (1,)))
    grad_input = grad_input.astype(BF).reshape(samples, node_count, emb_width).transpose(1, 0, 2)
    table_grad = send_and_scatter(
        back_source,
        source_slot,
        picks,
        bag_sizes,
        grad_input,
        tables.shape[0],
        node_count,
        lane_count,
        capacity,
    )
    crossed = crossed.reshape(samples, node_count, emb_width).transpose(1, 0, 2)
    return (crossed, hidden, table_grad)


def solution(mesh):
    return jax.shard_map(
        on_device,
        mesh=mesh,
        in_specs=(
            P(),
            P(("node", "local"), None),
            P(("node", "local"), None, None),
            P(("node", "local"), None),
            P("local", None, None),
            P(None, "local", None),
            P("local", None),
            P("local", None, None),
            P(),
            P("node", None),
        ),
        out_specs=(P("local", "node", None), P("node", "local"), P(("node", "local"), None)),
        check_vma=False,
    )
```

```python
import functools

import jax
import jax.numpy as jnp
from jax import lax
from jax.experimental import pallas as pl
from jax.experimental.pallas import tpu as pltpu
from jax.sharding import PartitionSpec as P

BF = jnp.bfloat16
F32 = jnp.float32
MESH = pl.DeviceIdType.MESH
PIECES = 4
HALVES = 2
BAG_GROUP = 32
LOW = 256


def dot(a, b, contract=((1,), (0,))):
    return lax.dot_general(a, b, (contract, ((), ())), preferred_element_type=F32)


def greet(n_node, n_local, node, lane):
    barrier = pltpu.get_barrier_semaphore()

    def by_node(k, carry):
        peer = lax.rem(node + k, n_node)
        pl.semaphore_signal(barrier, inc=1, device_id=(peer, lane), device_id_type=MESH)
        return carry

    def by_lane(d, carry):
        peer = lax.rem(lane + d, n_local)
        pl.semaphore_signal(barrier, inc=1, device_id=(node, peer), device_id_type=MESH)
        return carry

    lax.fori_loop(1, n_node, by_node, 0)
    lax.fori_loop(1, n_local, by_lane, 0)
    pl.semaphore_wait(barrier, n_node + n_local - 2)


def flatten_picks(idx_ref, size_ref, iota_ref, key_ref, low_ref):
    iota_ref[...] = lax.broadcasted_iota(jnp.int32, iota_ref.shape, 0).astype(F32).astype(BF)
    lanes = lax.broadcasted_iota(jnp.int32, (1, 128), 1)
    depth = lax.broadcasted_iota(jnp.int32, (8, 128), 0)

    def eight_groups(b, carry):
        rows = [[], []]
        for half in range(2):
            off = pl.multiple_of(b * 256 + half * 128, 128)
            picks = jnp.where(depth < size_ref[:, pl.ds(off, 128)], idx_ref[:, pl.ds(off, 128)], -1)
            turned = [picks] + [pltpu.roll(picks, 32 * d, 1) for d in (1, 2, 3)]
            for group in range(4):
                for h in range(2):
                    row = turned[(3 - group) % 4][4 * h + 3 : 4 * h + 4]
                    for q in (2, 1, 0):
                        source = turned[(q - group) % 4][4 * h + q : 4 * h + q + 1]
                        row = jnp.where(lanes < 32 * (q + 1), source, row)
                    rows[h].append(row)
        here = pl.ds(pl.multiple_of(b * 8, 8), 8)
        for h in range(2):
            picks = jnp.concatenate(rows[h], 0)
            key_ref[here, h * 128 : (h + 1) * 128] = ((picks >> 8) * 32 + (lanes & 31)).astype(F32)
            low_ref[here, h * 128 : (h + 1) * 128] = (picks & 255).astype(F32)
        return carry

    lax.fori_loop(0, idx_ref.shape[1] // 256, eight_groups, 0)


def count_group(key_ref, low_ref, iota_ref, group):
    iota = iota_ref[...]
    one, zero = jnp.ones((), BF), jnp.zeros((), BF)
    hot = []
    for ref in (key_ref, low_ref):
        row = jnp.broadcast_to(ref[pl.ds(group, 1), :], (16, LOW)).astype(BF)
        hot.append(jnp.where(jnp.concatenate([row] * 16, 0) == iota, one, zero))
    return dot(hot[0], hot[1], ((1,), (1,))).astype(BF)


def put_counts(count_ref, where, row, counts):
    for h in range(8):
        columns = slice(h * LOW, (h + 1) * LOW)
        if where is None:
            count_ref[pl.ds(row, BAG_GROUP), columns] = counts[h * 32 : (h + 1) * 32]
        else:
            count_ref[where, pl.ds(row, BAG_GROUP), columns] = counts[h * 32 : (h + 1) * 32]


def pool_kernel(
    n_node, n_local, pick_ref, slot_ref, idx_ref, size_ref, table_ref, x_ref,
    iota, key, low, counts, pooled, packed, node_send, node_recv, lane_send, lane_recv, *places,
):
    node, lane = lax.axis_index("node"), lax.axis_index("local")
    arrived, landed = places[:PIECES], places[PIECES:]
    cap = packed.shape[2]
    rows = pooled.shape[2]
    per_node = PIECES * rows // BAG_GROUP
    greet(n_node, n_local, node, lane)
    flatten_picks(idx_ref, size_ref, iota, key, low)

    def to_node(p, k):
        return pltpu.make_async_remote_copy(
            src_ref=pooled.at[p, k],
            dst_ref=arrived[p].at[node],
            send_sem=node_send.at[p, k],
            recv_sem=node_recv.at[p, k],
            device_id=(lax.rem(node + k, n_node), lane),
            device_id_type=MESH,
        )

    def to_lane(p, d):
        return pltpu.make_async_remote_copy(
            src_ref=packed.at[p, d],
            dst_ref=landed[p].at[pl.ds(lane * cap, cap)],
            send_sem=lane_send.at[p, d],
            recv_sem=lane_recv.at[p, d],
            device_id=(node, lax.rem(lane + d, n_local)),
            device_id_type=MESH,
        )

    def pool_piece(p):
        def four_nodes(c, carry):
            for i in range(16):
                source = lax.rem(node + c * 4 + i // 4, n_node)
                group = source * per_node + p * 4 + i % 4
                put_counts(counts, None, i * BAG_GROUP, count_group(key, low, iota, group))
            sums = dot(counts[...], table_ref[...]).astype(BF)
            for i in range(4):
                pooled[p, c * 4 + i] = sums[i * rows : (i + 1) * rows]

            for piece in range(PIECES):

                @pl.when(p == piece)
                def _():
                    def send(k, inner):
                        to_node(piece, k).start()
                        return inner

                    lax.fori_loop(jnp.maximum(c * 4, 1), c * 4 + 4, send, 0)

            return carry

        lax.fori_loop(0, n_node // 4, four_nodes, 0)

    def pack_piece(p):
        def arrive(k, carry):
            to_node(p, k).wait_recv()
            return carry

        lax.fori_loop(1, n_node, arrive, 0)
        arrived[p][node] = pooled[p, 0]
        for c in range(cap):
            landed[p][lane * cap + c] = arrived[p][pick_ref[lane * cap + c]]

        def send(d, carry):
            target = lax.rem(lane + d, n_local)
            for c in range(cap):
                packed[p, d, c] = arrived[p][pick_ref[target * cap + c]]
            to_lane(p, d).start()
            return carry

        lax.fori_loop(1, n_local, send, 0)

    def unpack_piece(p):
        def land(d, carry):
            to_lane(p, d).wait_recv()
            return carry

        lax.fori_loop(1, n_local, land, 0)
        for q in range(n_node):
            x_ref[p * rows : (p + 1) * rows, q * 128 : (q + 1) * 128] = landed[p][slot_ref[q]]

    def turn(p, carry):
        pool_piece(p)
        for piece in range(PIECES - 1):

            @pl.when(p == piece + 1)
            def _():
                pack_piece(piece)

        return carry

    lax.fori_loop(0, PIECES, turn, 0)
    pack_piece(PIECES - 1)

    for p in range(PIECES):
        unpack_piece(p)

        def sent_node(k, inner):
            to_node(p, k).wait_send()
            return inner

        def sent_lane(d, inner):
            to_lane(p, d).wait_send()
            return inner

        lax.fori_loop(1, n_node, sent_node, 0)
        lax.fori_loop(1, n_local, sent_lane, 0)


def scatter_kernel(
    n_node, n_local, pick_ref, slot_ref, idx_ref, size_ref, grad_ref, out_ref,
    iota, key, low, counts, packed, routed, home, home_t, total, lane_send, lane_recv, node_send, node_recv, *landed,
):
    node, lane = lax.axis_index("node"), lax.axis_index("local")
    cap = packed.shape[2]
    rows = packed.shape[3]
    per_node = PIECES * rows // BAG_GROUP
    greet(n_node, n_local, node, lane)

    def to_lane(p, d):
        return pltpu.make_async_remote_copy(
            src_ref=packed.at[p, d],
            dst_ref=landed[p].at[pl.ds(lane * cap, cap)],
            send_sem=lane_send.at[p, d],
            recv_sem=lane_recv.at[p, d],
            device_id=(node, lax.rem(lane + d, n_local)),
            device_id_type=MESH,
        )

    def to_node(p, k):
        return pltpu.make_async_remote_copy(
            src_ref=routed.at[p, k],
            dst_ref=home.at[p, node],
            send_sem=node_send.at[p, k],
            recv_sem=node_recv.at[p, k],
            device_id=(lax.rem(node + k, n_node), lane),
            device_id_type=MESH,
        )

    def pack_piece(p):
        here = slice(p * rows, (p + 1) * rows)

        def send(d, inner):
            target = lax.rem(lane + d, n_local)
            for c in range(cap):
                packed[p, d, c] = grad_ref[pick_ref[target * cap + c], here]
            to_lane(p, d).start()
            return inner

        lax.fori_loop(1, n_local, send, 0)
        for c in range(cap):
            landed[p][lane * cap + c] = grad_ref[pick_ref[lane * cap + c], here]

    def count_piece(p):
        def four_nodes(c, carry):
            for i in range(16):
                group = (c * 4 + i // 4) * per_node + p * 4 + i % 4
                row = pl.multiple_of(c * 16 * BAG_GROUP + i * BAG_GROUP, BAG_GROUP)
                put_counts(counts, p, row, count_group(key, low, iota, group))
            return carry

        lax.fori_loop(0, n_node // 4, four_nodes, 0)

    def route_piece(p):
        def land(d, carry):
            to_lane(p, d).wait_recv()
            return carry

        lax.fori_loop(1, n_local, land, 0)

        def send(k, carry):
            routed[p, k] = landed[p][slot_ref[lax.rem(node + k, n_node)]]
            to_node(p, k).start()
            return carry

        lax.fori_loop(1, n_node, send, 0)
        home[p, node] = landed[p][slot_ref[node]]

    def add_piece(p):
        def arrive(k, carry):
            to_node(p, k).wait_recv()
            return carry

        lax.fori_loop(1, n_node, arrive, 0)
        for n in range(n_node):
            home_t[:, n * rows : (n + 1) * rows] = home[p, n].T

        def columns(c, carry):
            here = pl.ds(pl.multiple_of(c * 512, 512), 512)
            total[:, here] += dot(home_t[...], counts[p, :, here])
            return carry

        lax.fori_loop(0, total.shape[1] // 512, columns, 0)

    for p in range(PIECES):
        pack_piece(p)
    flatten_picks(idx_ref, size_ref, iota, key, low)
    total[...] = jnp.zeros_like(total)

    def turn(p, carry):
        @pl.when(p < PIECES)
        def _():
            count_piece(p)

        for piece in range(PIECES):

            @pl.when(p == piece + 2)
            def _():
                route_piece(piece)

        @pl.when(p >= 3)
        def _():
            add_piece(p - 3)

        return carry

    lax.fori_loop(0, PIECES + 3, turn, 0)
    for n in range(total.shape[1] // 128):
        out_ref[n * 128 : (n + 1) * 128, :] = total[:, n * 128 : (n + 1) * 128].T

    for p in range(PIECES):

        def sent_node(k, inner):
            to_node(p, k).wait_send()
            return inner

        def sent_lane(d, inner):
            to_lane(p, d).wait_send()
            return inner

        lax.fori_loop(1, n_node, sent_node, 0)
        lax.fori_loop(1, n_local, sent_lane, 0)


def layer_kernel(
    n_local, x_ref, bias_ref, hbias_ref, grad_hbm, down_hbm, up_hbm, weight_hbm, crossed_ref, hidden_ref, gx_ref,
    down, up, weight, hgrad, term, gcross, inner, rank_send, rank_recv, rank, sib_send, sib_recv, pre_send, pre_recv,
    pre_own, gpre, load_sem, rank_ss, rank_rs, share_ss, share_rs, sib_ss, sib_rs, pre_ss, pre_rs, gp_ss, gp_rs,
    fw_ss, fw_rs,
):
    node, lane = lax.axis_index("node"), lax.axis_index("local")
    chips = n_local // 2
    chip, core = lane // 2, lax.rem(lane, 2)
    sibling = chip * 2 + 1 - core
    half = x_ref.shape[0] // HALVES
    share = half // n_local
    width = gpre.shape[3]
    total = x_ref.shape[1]

    def rows(h):
        return slice(h * half, (h + 1) * half)

    def remote(src, dst, send, recv, peer):
        return pltpu.make_async_remote_copy(
            src_ref=src, dst_ref=dst, send_sem=send, recv_sem=recv, device_id=(node, peer), device_id_type=MESH
        )

    def part_to(w, h, d):
        peer = lax.rem(lane + d, n_local)
        return remote(
            rank_send.at[w, h, peer], rank_recv.at[w, h, lane], rank_ss.at[w, h, d], rank_rs.at[w, h, d], peer
        )

    def share_to(w, h, d):
        peer = lax.rem(lane + d, n_local)
        return remote(rank.at[w, h, lane], rank.at[w, h, lane], share_ss.at[w, h, d], share_rs.at[w, h, d], peer)

    def to_sibling(h, y):
        return remote(sib_send.at[h, y], sib_recv.at[h, y], sib_ss.at[h, y], sib_rs.at[h, y], sibling)

    def pre_to(h, dy):
        peer = lax.rem(chip + dy, chips) * 2 + core
        return remote(pre_send.at[h, dy], pre_recv.at[h, dy], pre_ss.at[h, dy], pre_rs.at[h, dy], peer)

    def gpre_to(h, dy):
        peer = lax.rem(chip + dy, chips) * 2 + core
        return remote(gpre.at[h, lane], gpre.at[h, lane], gp_ss.at[h, dy], gp_rs.at[h, dy], peer)

    def forward(h, dy):
        source = lax.rem(chip + chips - dy, chips) * 2 + core
        return remote(gpre.at[h, source], gpre.at[h, source], fw_ss.at[h, dy], fw_rs.at[h, dy], sibling)

    def each(count, act, first=0):
        def body(i, carry):
            act(i)
            return carry

        lax.fori_loop(first, count, body, 0)

    my_columns = pl.ds(pl.multiple_of(lane * width, width), width)
    loads = [
        pltpu.make_async_copy(down_hbm, down, load_sem.at[0]),
        pltpu.make_async_copy(up_hbm, up, load_sem.at[1]),
        pltpu.make_async_copy(weight_hbm, weight, load_sem.at[2]),
        pltpu.make_async_copy(grad_hbm.at[:, my_columns], hgrad, load_sem.at[3]),
    ]
    for load in loads:
        load.start()

    barrier = pltpu.get_barrier_semaphore()
    each(
        n_local,
        lambda d: pl.semaphore_signal(
            barrier, inc=1, device_id=(node, lax.rem(lane + d, n_local)), device_id_type=MESH
        ),
        1,
    )
    pl.semaphore_wait(barrier, n_local - 1)

    def send_parts(w, h, part):
        def columns(n):
            here = pl.ds(pl.multiple_of(n * 256, 256), 256)
            piece = part(here).astype(BF)
            for t in range(n_local):
                rank_send[w, h, t, :, here] = piece[t * share : (t + 1) * share]

        each(rank.shape[4] // 256, columns)
        each(n_local, lambda d: part_to(w, h, d).start(), 1)

    def reduce_parts(w, h):
        rank_recv[w, h, lane] = rank_send[w, h, lane]
        each(n_local, lambda d: part_to(w, h, d).wait_recv(), 1)
        summed = rank_recv[w, h, 0].astype(F32)
        for t in range(1, n_local):
            summed = summed + rank_recv[w, h, t].astype(F32)
        rank[w, h, lane] = summed.astype(BF)
        each(n_local, lambda d: share_to(w, h, d).start(), 1)

    def whole_rank(w, h):
        return rank[w, h].reshape(half, rank.shape[4])

    def cross(h):
        each(n_local, lambda d: share_to(0, h, d).wait_recv(), 1)

        def columns(n):
            here = pl.ds(pl.multiple_of(n * 256, 256), 256)
            added = dot(whole_rank(0, h), up[:, here]) + bias_ref[:, here]
            x = x_ref[rows(h), here].astype(F32)
            result = (x * added + x).astype(BF)
            term[rows(h), here] = added
            inner[rows(h), here] = result
            for i in range(2):
                crossed_ref[n * 2 + i, rows(h), :] = result[:, i * 128 : (i + 1) * 128]

        each(total // 256, columns)

    def pre(h):
        def part(t):
            return dot(inner[rows(h), :], weight[:, pl.ds(pl.multiple_of(t * width, width), width)])

        def other_core(y):
            sib_send[h, y] = part(y * 2 + 1 - core).astype(BF)
            to_sibling(h, y).start()

        def my_core(i):
            dy = lax.rem(i + 1, chips)
            y = lax.rem(chip + dy, chips)
            mine = part(y * 2 + core)
            to_sibling(h, y).wait_recv()
            mine = mine + sib_recv[h, y].astype(F32)

            @pl.when(dy == 0)
            def _():
                pre_own[h] = mine

            @pl.when(dy > 0)
            def _():
                pre_send[h, dy] = mine.astype(BF)
                pre_to(h, dy).start()

        each(chips, other_core)
        each(chips, my_core)

    def activate(h):
        value = pre_own[h] + hbias_ref[:, my_columns]
        for dy in range(1, chips):
            pre_to(h, dy).wait_recv()
            value = value + pre_recv[h, dy].astype(F32)
        sig = jax.nn.sigmoid(value)
        hidden_ref[rows(h), :] = (value * sig).astype(BF)
        gpre[h, lane] = (hgrad[rows(h), :].astype(F32) * sig * (1.0 + value * (1.0 - sig))).astype(BF)
        each(chips, lambda dy: gpre_to(h, dy).start(), 1)
        forward(h, 0).start()

    def pass_on(h):
        def one(dy):
            gpre_to(h, dy).wait_recv()
            forward(h, dy).start()

        each(chips, one, 1)

    def back_chip(h, dy):
        forward(h, dy).wait_recv()
        y = lax.rem(chip + chips - dy, chips)
        grads = jnp.concatenate([gpre[h, y * 2], gpre[h, y * 2 + 1]], 1)
        wide = pl.ds(pl.multiple_of(y * 2 * width, 2 * width), 2 * width)

        def columns(n):
            here = pl.ds(pl.multiple_of(n * 256, 256), 256)
            added = dot(grads, weight[here, wide], ((1,), (1,)))
            if dy == 0:
                gcross[rows(h), here] = added
            else:
                gcross[rows(h), here] += added

        each(total // 256, columns)

    def rank_grad(h):
        inner[rows(h), :] = (gcross[rows(h), :] * x_ref[rows(h), :].astype(F32)).astype(BF)
        send_parts(1, h, lambda here: dot(inner[rows(h), :], up[here, :], ((1,), (1,))))

    def input_grad(h):
        each(n_local, lambda d: share_to(1, h, d).wait_recv(), 1)

        def columns(n):
            here = pl.ds(pl.multiple_of(n * 256, 256), 256)
            grads = gcross[rows(h), here]
            result = grads * term[rows(h), here] + grads + dot(whole_rank(1, h), down[here, :], ((1,), (1,)))
            result = result.astype(BF)
            for i in range(2):
                gx_ref[n * 2 + i, rows(h), :] = result[:, i * 128 : (i + 1) * 128]

        each(total // 256, columns)

    loads[0].wait()
    for h in range(HALVES):
        send_parts(0, h, lambda here: dot(x_ref[rows(h), :], down[:, here]))
    for h in range(HALVES):
        reduce_parts(0, h)
    loads[1].wait()
    for h in range(HALVES):
        cross(h)
        if h == 0:
            loads[2].wait()
        pre(h)
    loads[3].wait()
    for h in range(HALVES):
        activate(h)
    back_chip(0, 0)
    pass_on(0)
    for h in range(HALVES):
        for dy in range(1, chips):
            back_chip(h, dy)
        if h + 1 < HALVES:
            pass_on(h + 1)
        rank_grad(h)
        if h + 1 < HALVES:
            back_chip(h + 1, 0)
    for h in range(HALVES):
        reduce_parts(1, h)
    for h in range(HALVES):
        input_grad(h)

    for h in range(HALVES):
        for w in range(2):
            each(n_local, lambda d: part_to(w, h, d).wait_send(), 1)
            each(n_local, lambda d: share_to(w, h, d).wait_send(), 1)
        each(chips, lambda y: to_sibling(h, y).wait_send())
        each(chips, lambda dy: pre_to(h, dy).wait_send(), 1)
        each(chips, lambda dy: gpre_to(h, dy).wait_send(), 1)
        each(chips, lambda dy: forward(h, dy).wait_send())


SMEM = pl.BlockSpec(memory_space=pltpu.SMEM)
VMEM = pl.BlockSpec(memory_space=pltpu.VMEM)
SEM = pltpu.SemaphoreType.DMA
ANY = pl.BlockSpec(memory_space=pl.ANY)


def pool_and_send(pick, slot, picks, sizes, tables, n_node, n_local, cap, samples):
    rows = samples // PIECES
    groups = picks.shape[1] // BAG_GROUP
    width = tables.shape[1]
    return pl.pallas_call(
        functools.partial(pool_kernel, n_node, n_local),
        out_shape=jax.ShapeDtypeStruct((samples, n_node * width), BF),
        in_specs=[SMEM, SMEM, VMEM, VMEM, VMEM],
        out_specs=VMEM,
        scratch_shapes=[
            pltpu.VMEM((LOW, LOW), BF),
            pltpu.VMEM((groups, LOW), F32),
            pltpu.VMEM((groups, LOW), F32),
            pltpu.VMEM((16 * BAG_GROUP, tables.shape[0]), BF),
            pltpu.VMEM((PIECES, n_node, rows, width), BF),
            pltpu.VMEM((PIECES, n_local, cap, rows, width), BF),
            SEM((PIECES, n_node)),
            SEM((PIECES, n_node)),
            SEM((PIECES, n_local)),
            SEM((PIECES, n_local)),
            *[pltpu.VMEM((n_node, rows, width), BF)] * PIECES,
            *[pltpu.VMEM((n_local * cap, rows, width), BF)] * PIECES,
        ],
        compiler_params=pltpu.CompilerParams(collective_id=0, has_side_effects=True, vmem_limit_bytes=48 << 20),
        name="pool_and_send",
    )(pick, slot, picks, sizes, tables)


def send_and_scatter(pick, slot, picks, sizes, grads, table_rows, n_node, n_local, cap):
    samples, width = grads.shape[1:]
    rows = samples // PIECES
    groups = picks.shape[1] // BAG_GROUP
    return pl.pallas_call(
        functools.partial(scatter_kernel, n_node, n_local),
        out_shape=jax.ShapeDtypeStruct((table_rows, width), F32),
        in_specs=[SMEM, SMEM, VMEM, VMEM, VMEM],
        out_specs=VMEM,
        scratch_shapes=[
            pltpu.VMEM((LOW, LOW), BF),
            pltpu.VMEM((groups, LOW), F32),
            pltpu.VMEM((groups, LOW), F32),
            pltpu.VMEM((PIECES, n_node * rows, table_rows), BF),
            pltpu.VMEM((PIECES, n_local, cap, rows, width), BF),
            pltpu.VMEM((PIECES, n_node, rows, width), BF),
            pltpu.VMEM((PIECES, n_node, rows, width), BF),
            pltpu.VMEM((width, n_node * rows), BF),
            pltpu.VMEM((width, table_rows), F32),
            SEM((PIECES, n_local)),
            SEM((PIECES, n_local)),
            SEM((PIECES, n_node)),
            SEM((PIECES, n_node)),
            *[pltpu.VMEM((n_local * cap, rows, width), BF)] * PIECES,
        ],
        compiler_params=pltpu.CompilerParams(collective_id=1, has_side_effects=True, vmem_limit_bytes=56 << 20),
        name="send_and_scatter",
    )(pick, slot, picks, sizes, grads)


def layers(x, bias, hidden_bias, hidden_grad, down, up, weight, features, n_local):
    samples, total = x.shape
    depth, hidden = down.shape[1], weight.shape[1]
    half, width, chips = samples // HALVES, hidden // n_local, n_local // 2
    parts = (2, HALVES, n_local, half // n_local, depth)
    return pl.pallas_call(
        functools.partial(layer_kernel, n_local),
        out_shape=[
            jax.ShapeDtypeStruct((features, samples, total // features), BF),
            jax.ShapeDtypeStruct((samples, width), BF),
            jax.ShapeDtypeStruct((features, samples, total // features), BF),
        ],
        in_specs=[VMEM, VMEM, VMEM, ANY, ANY, ANY, ANY],
        out_specs=[VMEM, VMEM, VMEM],
        scratch_shapes=[
            pltpu.VMEM(down.shape, BF),
            pltpu.VMEM(up.shape, BF),
            pltpu.VMEM(weight.shape, BF),
            pltpu.VMEM((samples, width), BF),
            pltpu.VMEM(x.shape, F32),
            pltpu.VMEM(x.shape, F32),
            pltpu.VMEM(x.shape, BF),
            pltpu.VMEM(parts, BF),
            pltpu.VMEM(parts, BF),
            pltpu.VMEM(parts, BF),
            pltpu.VMEM((HALVES, chips, half, width), BF),
            pltpu.VMEM((HALVES, chips, half, width), BF),
            pltpu.VMEM((HALVES, chips, half, width), BF),
            pltpu.VMEM((HALVES, chips, half, width), BF),
            pltpu.VMEM((HALVES, half, width), F32),
            pltpu.VMEM((HALVES, n_local, half, width), BF),
            SEM((4,)),
            SEM((2, HALVES, n_local)),
            SEM((2, HALVES, n_local)),
            SEM((2, HALVES, n_local)),
            SEM((2, HALVES, n_local)),
            SEM((HALVES, chips)),
            SEM((HALVES, chips)),
            SEM((HALVES, chips)),
            SEM((HALVES, chips)),
            SEM((HALVES, chips)),
            SEM((HALVES, chips)),
            SEM((HALVES, chips)),
            SEM((HALVES, chips)),
        ],
        compiler_params=pltpu.CompilerParams(collective_id=2, has_side_effects=True, vmem_limit_bytes=56 << 20),
        name="layers",
    )(x, bias, hidden_bias, hidden_grad, down, up, weight)


def on_device(
    owner_map,
    bag_sizes,
    indices,
    tables,
    cross_down,
    cross_up,
    cross_bias,
    mlp_weight,
    mlp_bias,
    hidden_grad,
):
    node_count = lax.axis_size("node")
    lane_count = lax.axis_size("local")
    my_lane = lax.axis_index("local")
    capacity = node_count // lane_count + 1
    slot_total = lane_count * capacity
    samples = hidden_grad.shape[0]
    hidden_width = hidden_grad.shape[1]
    picks = indices[0].T
    feat_ids = jnp.arange(owner_map.shape[0], dtype=jnp.int32)
    node_ids = jnp.arange(node_count, dtype=jnp.int32)
    source_dev = node_ids * lane_count + my_lane
    source_feat = jnp.sum(
        jnp.where(owner_map[None, :] == source_dev[:, None], feat_ids[None, :], 0), axis=1
    )
    source_group = source_feat // node_count
    same_group = source_group[:, None] == source_group[None, :]
    earlier = node_ids[None, :] < node_ids[:, None]
    source_slot = source_group * capacity + jnp.sum(
        (same_group & earlier).astype(jnp.int32), axis=1
    )
    group_owners = lax.dynamic_slice_in_dim(owner_map, my_lane * node_count, node_count)
    owner_lane = group_owners % lane_count
    owner_node = group_owners // lane_count
    ahead_same = (owner_lane[:, None] == owner_lane[None, :]) & (
        owner_node[None, :] < owner_node[:, None]
    )
    owner_slot = owner_lane * capacity + jnp.sum(ahead_same.astype(jnp.int32), axis=1)
    slot_ids = jnp.arange(slot_total, dtype=jnp.int32)
    pick_source = jnp.sum(
        jnp.where(source_slot[None, :] == slot_ids[:, None], node_ids[None, :], 0), axis=1
    )
    back_source = jnp.sum(
        jnp.where(owner_slot[None, :] == slot_ids[:, None], node_ids[None, :], 0), axis=1
    )

    x_zero = pool_and_send(
        pick_source, owner_slot, picks, bag_sizes, tables, node_count, lane_count, capacity, samples
    )
    down = cross_down.reshape(-1, cross_down.shape[2])
    up = cross_up.reshape(cross_up.shape[0], -1)
    weight = mlp_weight.reshape(-1, hidden_width)
    crossed, hidden, grad_input = layers(
        x_zero,
        cross_bias.reshape(1, -1),
        mlp_bias.reshape(1, -1),
        hidden_grad,
        down,
        up,
        weight,
        node_count,
        lane_count,
    )
    table_grad = send_and_scatter(
        back_source,
        source_slot,
        picks,
        bag_sizes,
        grad_input,
        tables.shape[0],
        node_count,
        lane_count,
        capacity,
    )
    return (crossed, hidden, table_grad)


def solution(mesh):
    return jax.shard_map(
        on_device,
        mesh=mesh,
        in_specs=(
            P(),
            P(("node", "local"), None),
            P(("node", "local"), None, None),
            P(("node", "local"), None),
            P("local", None, None),
            P(None, "local", None),
            P("local", None),
            P("local", None, None),
            P(),
            P("node", None),
        ),
        out_specs=(P("local", "node", None), P("node", "local"), P(("node", "local"), None)),
        check_vma=False,
    )
```

```python
import functools
import types

import jax
import jax.numpy as jnp
from jax import lax
from jax.experimental import pallas as pl
from jax.experimental.pallas import tpu as pltpu
from jax.sharding import PartitionSpec as P

BF = jnp.bfloat16
F32 = jnp.float32
MESH = pl.DeviceIdType.MESH
PIECES = 4
HALVES = 2
CHUNK = 16
VMEM_LIMIT = 62 << 20
BAG_GROUP = 32
LOW = 256


def dot(a, b, contract=((1,), (0,))):
    return lax.dot_general(a, b, (contract, ((), ())), preferred_element_type=F32)


def greet(n_node, n_local, node, lane):
    barrier = pltpu.get_barrier_semaphore()

    def by_node(k, carry):
        peer = lax.rem(node + k, n_node)
        pl.semaphore_signal(barrier, inc=1, device_id=(peer, lane), device_id_type=MESH)
        return carry

    def by_lane(d, carry):
        peer = lax.rem(lane + d, n_local)
        pl.semaphore_signal(barrier, inc=1, device_id=(node, peer), device_id_type=MESH)
        return carry

    lax.fori_loop(1, n_node, by_node, 0)
    lax.fori_loop(1, n_local, by_lane, 0)
    pl.semaphore_wait(barrier, n_node + n_local - 2)


def flatten_picks(idx_ref, size_ref, iota_ref, key_ref, low_ref):
    iota_ref[...] = lax.broadcasted_iota(jnp.int32, iota_ref.shape, 0).astype(F32).astype(BF)
    lanes = lax.broadcasted_iota(jnp.int32, (1, 128), 1)
    depth = lax.broadcasted_iota(jnp.int32, (8, 128), 0)

    def eight_groups(b, carry):
        rows = [[], []]
        for half in range(2):
            off = pl.multiple_of(b * 256 + half * 128, 128)
            picks = jnp.where(depth < size_ref[:, pl.ds(off, 128)], idx_ref[:, pl.ds(off, 128)], -1)
            turned = [picks] + [pltpu.roll(picks, 32 * d, 1) for d in (1, 2, 3)]
            for group in range(4):
                for h in range(2):
                    row = turned[(3 - group) % 4][4 * h + 3 : 4 * h + 4]
                    for q in (2, 1, 0):
                        source = turned[(q - group) % 4][4 * h + q : 4 * h + q + 1]
                        row = jnp.where(lanes < 32 * (q + 1), source, row)
                    rows[h].append(row)
        here = pl.ds(pl.multiple_of(b * 8, 8), 8)
        for h in range(2):
            picks = jnp.concatenate(rows[h], 0)
            key_ref[here, h * 128 : (h + 1) * 128] = ((picks >> 8) * 32 + (lanes & 31)).astype(F32)
            low_ref[here, h * 128 : (h + 1) * 128] = (picks & 255).astype(F32)
        return carry

    lax.fori_loop(0, idx_ref.shape[1] // 256, eight_groups, 0)


def count_group(key_ref, low_ref, iota_ref, group):
    iota = iota_ref[...]
    one, zero = jnp.ones((), BF), jnp.zeros((), BF)
    hot = []
    for ref in (key_ref, low_ref):
        row = jnp.broadcast_to(ref[pl.ds(group, 1), :], (16, LOW)).astype(BF)
        hot.append(jnp.where(jnp.concatenate([row] * 16, 0) == iota, one, zero))
    return dot(hot[0], hot[1], ((1,), (1,))).astype(BF)


def put_counts(count_ref, where, row, counts):
    for h in range(8):
        count_ref[where, pl.ds(row, BAG_GROUP), h * LOW : (h + 1) * LOW] = counts[h * 32 : (h + 1) * 32]


def step_kernel(names, n_node, n_local, *refs):
    r = types.SimpleNamespace(**dict(zip(names, refs)))
    node, lane = lax.axis_index("node"), lax.axis_index("local")
    chips = n_local // 2
    chip, core = lane // 2, lax.rem(lane, 2)
    sibling = chip * 2 + 1 - core
    cap, small = r.packed.shape[2], r.packed.shape[3]
    samples, total = r.x.shape
    half = samples // HALVES
    share = half // n_local
    width = r.gpre.shape[3]
    per_node = samples // BAG_GROUP
    chunks = n_node * small // (CHUNK * BAG_GROUP)
    arrived = [getattr(r, f"arrived{p}") for p in range(PIECES)]
    landed = [getattr(r, f"landed{p}") for p in range(PIECES)]
    returned = [getattr(r, f"returned{p}") for p in range(PIECES)]

    def rows(h):
        return slice(h * half, (h + 1) * half)

    def each(count, act, first=0):
        def body(i, carry):
            act(i)
            return carry

        lax.fori_loop(first, count, body, 0)

    def remote(src, dst, sems, at, peer):
        send, recv = sems
        return pltpu.make_async_remote_copy(
            src_ref=src, dst_ref=dst, send_sem=send.at[at], recv_sem=recv.at[at], device_id=peer, device_id_type=MESH
        )

    def node_peer(k):
        return lax.rem(node + k, n_node), lane

    def lane_peer(d):
        return node, lax.rem(lane + d, n_local)

    def chip_peer(dy):
        return node, lax.rem(chip + dy, chips) * 2 + core

    def out_node(p, k):
        return remote(r.pooled.at[p, k], arrived[p].at[node], (r.on_s, r.on_r), (p, k), node_peer(k))

    def out_lane(p, d):
        here = pl.ds(lane * cap, cap)
        return remote(r.packed.at[p, d], landed[p].at[here], (r.ol_s, r.ol_r), (p, d), lane_peer(d))

    def back_lane(p, d):
        here = pl.ds(lane * cap, cap)
        return remote(r.packed.at[p, d], returned[p].at[here], (r.bl_s, r.bl_r), (p, d), lane_peer(d))

    def back_node(p, k):
        return remote(r.pooled.at[p, k], r.home.at[p, node], (r.bn_s, r.bn_r), (p, k), node_peer(k))

    def part_to(w, h, d):
        peer = lane_peer(d)
        return remote(r.rank_send.at[w, h, peer[1]], r.rank_recv.at[w, h, lane], (r.rk_s, r.rk_r), (w, h, d), peer)

    def share_to(w, h, d):
        return remote(r.rank.at[w, h, lane], r.rank.at[w, h, lane], (r.sh_s, r.sh_r), (w, h, d), lane_peer(d))

    def to_sibling(h, y):
        return remote(r.sib_send.at[h, y], r.sib_recv.at[h, y], (r.sb_s, r.sb_r), (h, y), (node, sibling))

    def pre_to(h, dy):
        return remote(r.pre_send.at[h, dy], r.pre_recv.at[h, dy], (r.pr_s, r.pr_r), (h, dy), chip_peer(dy))

    def gpre_to(h, dy):
        return remote(r.gpre.at[h, lane], r.gpre.at[h, lane], (r.gp_s, r.gp_r), (h, dy), chip_peer(dy))

    def forward(h, dy):
        source = lax.rem(chip + chips - dy, chips) * 2 + core
        return remote(r.gpre.at[h, source], r.gpre.at[h, source], (r.fw_s, r.fw_r), (h, dy), (node, sibling))

    def save(t):
        buffer = lax.rem(t, 2)
        return pltpu.make_async_copy(r.counts.at[buffer], r.kept.at[t], r.save_sem.at[buffer])

    def fetch(t):
        buffer = lax.rem(t, 2)
        return pltpu.make_async_copy(r.kept.at[t], r.counts.at[buffer], r.fetch_sem.at[buffer])

    def pool_piece(p):
        def one_chunk(c):
            t = p * chunks + c

            @pl.when(t >= 2)
            def _():
                save(t - 2).wait()

            buffer = lax.rem(t, 2)
            for i in range(CHUNK):
                source = lax.rem(node + c * 4 + i // 4, n_node)
                group = source * per_node + p * 4 + i % 4
                put_counts(r.counts, buffer, i * BAG_GROUP, count_group(r.key, r.low, r.iota, group))
            save(t).start()
            sums = dot(r.counts[buffer], r.table[...]).astype(BF)
            for i in range(4):
                r.pooled[p, c * 4 + i] = sums[i * small : (i + 1) * small]
            for piece in range(PIECES):

                @pl.when(p == piece)
                def _():
                    each(c * 4 + 4, lambda k: out_node(piece, k).start(), jnp.maximum(c * 4, 1))

        each(chunks, one_chunk)

    def pack_piece(p):
        each(n_node, lambda k: out_node(p, k).wait_recv(), 1)
        arrived[p][node] = r.pooled[p, 0]

        def send(d):
            target = lax.rem(lane + d, n_local)
            for c in range(cap):
                r.packed[p, d, c] = arrived[p][r.pick[target * cap + c]]
            out_lane(p, d).start()

        each(n_local, send, 1)
        for c in range(cap):
            landed[p][lane * cap + c] = arrived[p][r.pick[lane * cap + c]]

    def unpack_piece(p):
        each(n_local, lambda d: out_lane(p, d).wait_recv(), 1)
        for q in range(n_node):
            r.x[p * small : (p + 1) * small, q * 128 : (q + 1) * 128] = landed[p][r.slot[q]]

    def send_parts(w, h, part):
        def columns(n):
            here = pl.ds(pl.multiple_of(n * 256, 256), 256)
            piece = part(here).astype(BF)
            for t in range(n_local):
                r.rank_send[w, h, t, :, here] = piece[t * share : (t + 1) * share]

        each(r.rank.shape[4] // 256, columns)
        each(n_local, lambda d: part_to(w, h, d).start(), 1)

    def reduce_parts(w, h):
        r.rank_recv[w, h, lane] = r.rank_send[w, h, lane]
        each(n_local, lambda d: part_to(w, h, d).wait_recv(), 1)
        summed = r.rank_recv[w, h, 0].astype(F32)
        for t in range(1, n_local):
            summed = summed + r.rank_recv[w, h, t].astype(F32)
        r.rank[w, h, lane] = summed.astype(BF)
        each(n_local, lambda d: share_to(w, h, d).start(), 1)

    def whole_rank(w, h):
        return r.rank[w, h].reshape(half, r.rank.shape[4])

    def side_by_side(ref, h):
        return jnp.concatenate([ref[q, rows(h), :] for q in range(n_node)], 1)

    def low_parts(h):
        send_parts(0, h, lambda here: dot(r.x[rows(h), :], r.down[:, here]))

    def cross(h):
        each(n_local, lambda d: share_to(0, h, d).wait_recv(), 1)

        def columns(n):
            here = pl.ds(pl.multiple_of(n * 512, 512), 512)
            added = dot(whole_rank(0, h), r.up[:, here]) + r.bias[:, here]
            x = r.x[rows(h), here].astype(F32)
            result = (x * added + x).astype(BF)
            r.term[rows(h), here] = added
            for i in range(4):
                r.crossed[n * 4 + i, rows(h), :] = result[:, i * 128 : (i + 1) * 128]

        each(total // 512, columns)

    def pre(h):
        def part(t):
            return dot(side_by_side(r.crossed, h), r.weight[:, pl.ds(pl.multiple_of(t * width, width), width)])

        def other_core(y):
            r.sib_send[h, y] = part(y * 2 + 1 - core).astype(BF)
            to_sibling(h, y).start()

        def my_core(i):
            dy = lax.rem(i + 1, chips)
            y = lax.rem(chip + dy, chips)
            mine = part(y * 2 + core)
            to_sibling(h, y).wait_recv()
            mine = mine + r.sib_recv[h, y].astype(F32)

            @pl.when(dy == 0)
            def _():
                r.pre_own[h] = mine

            @pl.when(dy > 0)
            def _():
                r.pre_send[h, dy] = mine.astype(BF)
                pre_to(h, dy).start()

        each(chips, other_core)
        each(chips, my_core)

    def activate(h):
        value = r.pre_own[h] + r.hbias[:, pl.ds(pl.multiple_of(lane * width, width), width)]
        for dy in range(1, chips):
            pre_to(h, dy).wait_recv()
            value = value + r.pre_recv[h, dy].astype(F32)
        sig = jax.nn.sigmoid(value)
        r.hidden[rows(h), :] = (value * sig).astype(BF)
        r.gpre[h, lane] = (r.hgrad[rows(h), :].astype(F32) * sig * (1.0 + value * (1.0 - sig))).astype(BF)
        each(chips, lambda dy: gpre_to(h, dy).start(), 1)
        forward(h, 0).start()

    def pass_on(h):
        def one(dy):
            gpre_to(h, dy).wait_recv()
            forward(h, dy).start()

        each(chips, one, 1)

    def back_chips(h, steps):
        sides = []
        for dy in steps:
            forward(h, dy).wait_recv()
            y = lax.rem(chip + chips - dy, chips)
            wide = pl.ds(pl.multiple_of(y * 2 * width, 2 * width), 2 * width)
            sides.append((y, wide))

        def columns(n):
            here = pl.ds(pl.multiple_of(n * 512, 512), 512)
            added = None
            for y, wide in sides:
                grads = jnp.concatenate([r.gpre[h, y * 2], r.gpre[h, y * 2 + 1]], 1)
                term = dot(grads, r.weight[here, wide], ((1,), (1,)))
                added = term if added is None else added + term
            if 0 in steps:
                r.gcross[rows(h), here] = added
            else:
                r.gcross[rows(h), here] += added

        each(total // 512, columns)

    def rank_grad(h):
        for q in range(n_node):
            here = slice(q * 128, (q + 1) * 128)
            r.gx[q, rows(h), :] = (r.gcross[rows(h), here] * r.x[rows(h), here].astype(F32)).astype(BF)
        send_parts(1, h, lambda here: dot(side_by_side(r.gx, h), r.up[here, :], ((1,), (1,))))

    def input_grad(h):
        each(n_local, lambda d: share_to(1, h, d).wait_recv(), 1)

        def columns(n):
            here = pl.ds(pl.multiple_of(n * 512, 512), 512)
            grads = r.gcross[rows(h), here]
            result = grads * r.term[rows(h), here] + grads + dot(whole_rank(1, h), r.down[here, :], ((1,), (1,)))
            result = result.astype(BF)
            for i in range(4):
                r.gx[n * 4 + i, rows(h), :] = result[:, i * 128 : (i + 1) * 128]

        each(total // 512, columns)

    def pack_back(p):
        here = slice(p * small, (p + 1) * small)
        each(n_local, lambda d: out_lane(p, d).wait_send(), 1)

        def send(d):
            target = lax.rem(lane + d, n_local)
            for c in range(cap):
                r.packed[p, d, c] = r.gx[r.back_pick[target * cap + c], here]
            back_lane(p, d).start()

        each(n_local, send, 1)
        for c in range(cap):
            returned[p][lane * cap + c] = r.gx[r.back_pick[lane * cap + c], here]

    def route_piece(p):
        each(n_node, lambda k: out_node(p, k).wait_send(), 1)
        each(n_local, lambda d: back_lane(p, d).wait_recv(), 1)

        def send(k):
            r.pooled[p, k] = returned[p][r.back_slot[lax.rem(node + k, n_node)]]
            back_node(p, k).start()

        each(n_node, send, 1)
        r.home[p, node] = returned[p][r.back_slot[node]]

    def add_piece(p):
        each(n_node, lambda k: back_node(p, k).wait_recv(), 1)

        def one_chunk(c):
            t = p * chunks + c
            buffer = lax.rem(t, 2)
            for i in range(4):
                r.home_t[:, i * small : (i + 1) * small] = r.home[p, lax.rem(node + c * 4 + i, n_node)].T
            fetch(t).wait()
            for n in range(r.sums.shape[1] // 512):
                here = slice(n * 512, (n + 1) * 512)
                r.sums[:, here] += dot(r.home_t[...], r.counts[buffer, :, here])

            @pl.when(t + 2 < PIECES * chunks)
            def _():
                fetch(t + 2).start()

        each(chunks, one_chunk)

    my_columns = pl.ds(pl.multiple_of(lane * width, width), width)
    loads = [
        pltpu.make_async_copy(r.down_hbm, r.down, r.load_sem.at[0]),
        pltpu.make_async_copy(r.up_hbm, r.up, r.load_sem.at[1]),
        pltpu.make_async_copy(r.weight_hbm, r.weight, r.load_sem.at[2]),
        pltpu.make_async_copy(r.grad_hbm.at[:, my_columns], r.hgrad, r.load_sem.at[3]),
    ]
    for load in loads:
        load.start()
    greet(n_node, n_local, node, lane)
    flatten_picks(r.idx, r.size, r.iota, r.key, r.low)
    r.sums[...] = jnp.zeros_like(r.sums)

    def turn(p):
        pool_piece(p)
        for piece in range(PIECES - 1):

            @pl.when(p == piece + 1)
            def _():
                pack_piece(piece)

    each(PIECES, turn)
    pack_piece(PIECES - 1)
    for t in range(2):
        save(PIECES * chunks - 2 + t).wait()
    for t in range(2):
        fetch(t).start()
    for load in loads:
        load.wait()
    per_half = PIECES // HALVES
    for h in range(HALVES):
        for p in range(h * per_half, (h + 1) * per_half):
            unpack_piece(p)
        low_parts(h)
    for h in range(HALVES):
        reduce_parts(0, h)
    for h in range(HALVES):
        cross(h)
        pre(h)
    for h in range(HALVES):
        activate(h)
    back_chips(0, [0])
    pass_on(0)
    back_chips(0, [1, 2, 3])
    pass_on(1)
    rank_grad(0)
    back_chips(1, [0, 1, 2, 3])
    reduce_parts(1, 0)
    rank_grad(1)
    input_grad(0)
    pack_back(0)
    pack_back(1)
    reduce_parts(1, 1)
    input_grad(1)
    pack_back(2)
    pack_back(3)
    route_piece(0)
    route_piece(1)
    add_piece(0)
    route_piece(2)
    add_piece(1)
    route_piece(3)
    add_piece(2)
    add_piece(3)
    for n in range(r.sums.shape[1] // 128):
        r.table_grad[n * 128 : (n + 1) * 128, :] = r.sums[:, n * 128 : (n + 1) * 128].T

    for p in range(PIECES):
        each(n_node, lambda k: back_node(p, k).wait_send(), 1)
        each(n_local, lambda d: back_lane(p, d).wait_send(), 1)
    for h in range(HALVES):
        for w in range(2):
            each(n_local, lambda d: part_to(w, h, d).wait_send(), 1)
            each(n_local, lambda d: share_to(w, h, d).wait_send(), 1)
        each(chips, lambda y: to_sibling(h, y).wait_send())
        each(chips, lambda dy: pre_to(h, dy).wait_send(), 1)
        each(chips, lambda dy: gpre_to(h, dy).wait_send(), 1)
        each(chips, lambda dy: forward(h, dy).wait_send())


SMEM = pl.BlockSpec(memory_space=pltpu.SMEM)
VMEM = pl.BlockSpec(memory_space=pltpu.VMEM)
ANY = pl.BlockSpec(memory_space=pl.ANY)
SEM = pltpu.SemaphoreType.DMA


def train_step(operands, features, samples, n_node, n_local, cap):
    depth, hidden = operands["down_hbm"].shape[1], operands["weight_hbm"].shape[1]
    total = operands["down_hbm"].shape[0]
    table_rows, emb = operands["table"].shape
    groups = operands["idx"].shape[1] // BAG_GROUP
    small, half, width, chips = samples // PIECES, samples // HALVES, hidden // n_local, n_local // 2
    kept = (groups // CHUNK, CHUNK * BAG_GROUP, table_rows)
    outs = {
        "crossed": (jax.ShapeDtypeStruct((features, samples, emb), BF), VMEM),
        "hidden": (jax.ShapeDtypeStruct((samples, width), BF), VMEM),
        "table_grad": (jax.ShapeDtypeStruct((table_rows, emb), F32), VMEM),
        "kept": (jax.ShapeDtypeStruct(kept, BF), ANY),
    }
    parts = pltpu.VMEM((2, HALVES, n_local, half // n_local, depth), BF)
    quarter = pltpu.VMEM((HALVES, chips, half, width), BF)
    scratch = {
        "iota": pltpu.VMEM((LOW, LOW), BF),
        "key": pltpu.VMEM((groups, LOW), F32),
        "low": pltpu.VMEM((groups, LOW), F32),
        "counts": pltpu.VMEM((2, *kept[1:]), BF),
        "pooled": pltpu.VMEM((PIECES, n_node, small, emb), BF),
        "packed": pltpu.VMEM((PIECES, n_local, cap, small, emb), BF),
        "home": pltpu.VMEM((PIECES, n_node, small, emb), BF),
        "home_t": pltpu.VMEM((emb, 4 * small), BF),
        "sums": pltpu.VMEM((emb, table_rows), F32),
        "x": pltpu.VMEM((samples, total), BF),
        "down": pltpu.VMEM((total, depth), BF),
        "up": pltpu.VMEM((depth, total), BF),
        "weight": pltpu.VMEM((total, hidden), BF),
        "hgrad": pltpu.VMEM((samples, width), BF),
        "term": pltpu.VMEM((samples, total), F32),
        "gcross": pltpu.VMEM((samples, total), F32),
        "gx": pltpu.VMEM((features, samples, emb), BF),
        "rank_send": parts,
        "rank_recv": parts,
        "rank": parts,
        "sib_send": quarter,
        "sib_recv": quarter,
        "pre_send": quarter,
        "pre_recv": quarter,
        "pre_own": pltpu.VMEM((HALVES, half, width), F32),
        "gpre": pltpu.VMEM((HALVES, n_local, half, width), BF),
        "load_sem": SEM((4,)),
        "save_sem": SEM((2,)),
        "fetch_sem": SEM((2,)),
    }
    for p in range(PIECES):
        scratch[f"arrived{p}"] = pltpu.VMEM((n_node, small, emb), BF)
        scratch[f"landed{p}"] = pltpu.VMEM((n_local * cap, small, emb), BF)
        scratch[f"returned{p}"] = pltpu.VMEM((n_local * cap, small, emb), BF)
    for names, shape in (
        (("on", "bn"), (PIECES, n_node)),
        (("ol", "bl"), (PIECES, n_local)),
        (("rk", "sh"), (2, HALVES, n_local)),
        (("sb", "pr", "gp", "fw"), (HALVES, chips)),
    ):
        for name in names:
            scratch[name + "_s"] = SEM(shape)
            scratch[name + "_r"] = SEM(shape)
    places = {"pick": SMEM, "slot": SMEM, "back_pick": SMEM, "back_slot": SMEM}
    specs = [places.get(name, ANY if name.endswith("_hbm") else VMEM) for name in operands]
    names = [*operands, *outs, *scratch]
    return pl.pallas_call(
        functools.partial(step_kernel, names, n_node, n_local),
        out_shape=[shape for shape, _ in outs.values()],
        in_specs=specs,
        out_specs=[spec for _, spec in outs.values()],
        scratch_shapes=list(scratch.values()),
        compiler_params=pltpu.CompilerParams(collective_id=0, has_side_effects=True, vmem_limit_bytes=VMEM_LIMIT),
        name="train_step",
    )(*operands.values())


def on_device(
    owner_map,
    bag_sizes,
    indices,
    tables,
    cross_down,
    cross_up,
    cross_bias,
    mlp_weight,
    mlp_bias,
    hidden_grad,
):
    node_count = lax.axis_size("node")
    lane_count = lax.axis_size("local")
    my_lane = lax.axis_index("local")
    capacity = node_count // lane_count + 1
    slot_total = lane_count * capacity
    samples = hidden_grad.shape[0]
    hidden_width = hidden_grad.shape[1]
    feat_ids = jnp.arange(owner_map.shape[0], dtype=jnp.int32)
    node_ids = jnp.arange(node_count, dtype=jnp.int32)
    source_dev = node_ids * lane_count + my_lane
    source_feat = jnp.sum(
        jnp.where(owner_map[None, :] == source_dev[:, None], feat_ids[None, :], 0), axis=1
    )
    source_group = source_feat // node_count
    same_group = source_group[:, None] == source_group[None, :]
    earlier = node_ids[None, :] < node_ids[:, None]
    source_slot = source_group * capacity + jnp.sum(
        (same_group & earlier).astype(jnp.int32), axis=1
    )
    group_owners = lax.dynamic_slice_in_dim(owner_map, my_lane * node_count, node_count)
    owner_lane = group_owners % lane_count
    owner_node = group_owners // lane_count
    ahead_same = (owner_lane[:, None] == owner_lane[None, :]) & (
        owner_node[None, :] < owner_node[:, None]
    )
    owner_slot = owner_lane * capacity + jnp.sum(ahead_same.astype(jnp.int32), axis=1)
    slot_ids = jnp.arange(slot_total, dtype=jnp.int32)
    pick_source = jnp.sum(
        jnp.where(source_slot[None, :] == slot_ids[:, None], node_ids[None, :], 0), axis=1
    )
    back_source = jnp.sum(
        jnp.where(owner_slot[None, :] == slot_ids[:, None], node_ids[None, :], 0), axis=1
    )

    operands = {
        "pick": pick_source,
        "slot": owner_slot,
        "back_pick": back_source,
        "back_slot": source_slot,
        "idx": indices[0].T,
        "size": bag_sizes,
        "table": tables,
        "bias": cross_bias.reshape(1, -1),
        "hbias": mlp_bias.reshape(1, -1),
        "grad_hbm": hidden_grad,
        "down_hbm": cross_down.reshape(-1, cross_down.shape[2]),
        "up_hbm": cross_up.reshape(cross_up.shape[0], -1),
        "weight_hbm": mlp_weight.reshape(-1, hidden_width),
    }
    crossed, hidden, table_grad, _ = train_step(operands, node_count, samples, node_count, lane_count, capacity)
    return (crossed, hidden, table_grad)


def solution(mesh):
    return jax.shard_map(
        on_device,
        mesh=mesh,
        in_specs=(
            P(),
            P(("node", "local"), None),
            P(("node", "local"), None, None),
            P(("node", "local"), None),
            P("local", None, None),
            P(None, "local", None),
            P("local", None),
            P("local", None, None),
            P(),
            P("node", None),
        ),
        out_specs=(P("local", "node", None), P("node", "local"), P(("node", "local"), None)),
        check_vma=False,
    )
```

```python
import functools
import types

import jax
import jax.numpy as jnp
from jax import lax
from jax.experimental import pallas as pl
from jax.experimental.pallas import tpu as pltpu
from jax.sharding import PartitionSpec as P

BF = jnp.bfloat16
F32 = jnp.float32
MESH = pl.DeviceIdType.MESH
PIECES = 8
HALVES = 2
CHUNK = 16
LAG = 3
VMEM_LIMIT = 62 << 20
BAG_GROUP = 32
LOW = 256


def dot(a, b, contract=((1,), (0,))):
    return lax.dot_general(a, b, (contract, ((), ())), preferred_element_type=F32)


def greet(n_node, n_local, node, lane):
    barrier = pltpu.get_barrier_semaphore()

    def by_node(k, carry):
        peer = lax.rem(node + k, n_node)
        pl.semaphore_signal(barrier, inc=1, device_id=(peer, lane), device_id_type=MESH)
        return carry

    def by_lane(d, carry):
        peer = lax.rem(lane + d, n_local)
        pl.semaphore_signal(barrier, inc=1, device_id=(node, peer), device_id_type=MESH)
        return carry

    lax.fori_loop(1, n_node, by_node, 0)
    lax.fori_loop(1, n_local, by_lane, 0)
    return barrier


def flatten_picks(idx_ref, size_ref, iota_ref, key_ref, low_ref):
    iota_ref[...] = lax.broadcasted_iota(jnp.int32, iota_ref.shape, 0).astype(F32).astype(BF)
    lanes = lax.broadcasted_iota(jnp.int32, (1, 128), 1)
    depth = lax.broadcasted_iota(jnp.int32, (8, 128), 0)

    def eight_groups(b, carry):
        rows = [[], []]
        for half in range(2):
            off = pl.multiple_of(b * 256 + half * 128, 128)
            picks = jnp.where(depth < size_ref[:, pl.ds(off, 128)], idx_ref[:, pl.ds(off, 128)], -1)
            turned = [picks] + [pltpu.roll(picks, 32 * d, 1) for d in (1, 2, 3)]
            for group in range(4):
                for h in range(2):
                    row = turned[(3 - group) % 4][4 * h + 3 : 4 * h + 4]
                    for q in (2, 1, 0):
                        source = turned[(q - group) % 4][4 * h + q : 4 * h + q + 1]
                        row = jnp.where(lanes < 32 * (q + 1), source, row)
                    rows[h].append(row)
        here = pl.ds(pl.multiple_of(b * 8, 8), 8)
        for h in range(2):
            picks = jnp.concatenate(rows[h], 0)
            key_ref[here, h * 128 : (h + 1) * 128] = ((picks >> 8) * 32 + (lanes & 31)).astype(F32)
            low_ref[here, h * 128 : (h + 1) * 128] = (picks & 255).astype(F32)
        return carry

    lax.fori_loop(0, idx_ref.shape[1] // 256, eight_groups, 0)


def count_group(key_ref, low_ref, iota_ref, group):
    iota = iota_ref[...]
    one, zero = jnp.ones((), BF), jnp.zeros((), BF)
    hot = []
    for ref in (key_ref, low_ref):
        row = jnp.broadcast_to(ref[pl.ds(group, 1), :], (16, LOW)).astype(BF)
        hot.append(jnp.where(jnp.concatenate([row] * 16, 0) == iota, one, zero))
    return dot(hot[0], hot[1], ((1,), (1,))).astype(BF)


def put_counts(count_ref, where, row, counts):
    for h in range(8):
        count_ref[where, pl.ds(row, BAG_GROUP), h * LOW : (h + 1) * LOW] = counts[h * 32 : (h + 1) * 32]


def step_kernel(names, n_node, n_local, *refs):
    r = types.SimpleNamespace(**dict(zip(names, refs)))
    node, lane = lax.axis_index("node"), lax.axis_index("local")
    chips = n_local // 2
    chip, core = lane // 2, lax.rem(lane, 2)
    sibling = chip * 2 + 1 - core
    cap, small = r.packed.shape[2], r.packed.shape[3]
    samples, total = r.x.shape
    half = samples // HALVES
    share = half // n_local
    width = r.gpre.shape[3]
    per_node = samples // BAG_GROUP
    groups = small // BAG_GROUP
    at_once = CHUNK // groups
    chunks = n_node // at_once
    arrived = [getattr(r, f"arrived{p}") for p in range(PIECES)]
    landed = [getattr(r, f"landed{p}") for p in range(PIECES)]
    returned = [getattr(r, f"returned{p}") for p in range(PIECES)]

    def rows(h):
        return slice(h * half, (h + 1) * half)

    def each(count, act, first=0):
        def body(i, carry):
            act(i)
            return carry

        lax.fori_loop(first, count, body, 0)

    def remote(src, dst, sems, at, peer):
        send, recv = sems
        return pltpu.make_async_remote_copy(
            src_ref=src, dst_ref=dst, send_sem=send.at[at], recv_sem=recv.at[at], device_id=peer, device_id_type=MESH
        )

    def node_peer(k):
        return lax.rem(node + k, n_node), lane

    def lane_peer(d):
        return node, lax.rem(lane + d, n_local)

    def chip_peer(dy):
        return node, lax.rem(chip + dy, chips) * 2 + core

    def out_node(p, k):
        return remote(r.pooled.at[p, k], arrived[p].at[node], (r.on_s, r.on_r), (p, k), node_peer(k))

    def out_lane(p, d):
        here = pl.ds(lane * cap, cap)
        return remote(r.packed.at[p, d], landed[p].at[here], (r.ol_s, r.ol_r), (p, d), lane_peer(d))

    def back_lane(p, d):
        here = pl.ds(lane * cap, cap)
        return remote(r.packed.at[p, d], returned[p].at[here], (r.bl_s, r.bl_r), (p, d), lane_peer(d))

    def back_node(p, k):
        return remote(r.pooled.at[p, k], r.home.at[p, node], (r.bn_s, r.bn_r), (p, k), node_peer(k))

    def part_to(w, h, d):
        peer = lane_peer(d)
        return remote(r.rank_send.at[w, h, peer[1]], r.rank_recv.at[w, h, lane], (r.rk_s, r.rk_r), (w, h, d), peer)

    def share_to(w, h, d):
        return remote(r.rank.at[w, h, lane], r.rank.at[w, h, lane], (r.sh_s, r.sh_r), (w, h, d), lane_peer(d))

    def to_sibling(h, y):
        return remote(r.sib_send.at[h, y], r.sib_recv.at[h, y], (r.sb_s, r.sb_r), (h, y), (node, sibling))

    def pre_to(h, dy):
        return remote(r.pre_send.at[h, dy], r.pre_recv.at[h, dy], (r.pr_s, r.pr_r), (h, dy), chip_peer(dy))

    def gpre_to(h, dy):
        return remote(r.gpre.at[h, lane], r.gpre.at[h, lane], (r.gp_s, r.gp_r), (h, dy), chip_peer(dy))

    def forward(h, dy):
        source = lax.rem(chip + chips - dy, chips) * 2 + core
        return remote(r.gpre.at[h, source], r.gpre.at[h, source], (r.fw_s, r.fw_r), (h, dy), (node, sibling))

    def save(t):
        buffer = lax.rem(t, 2)
        return pltpu.make_async_copy(r.counts.at[buffer], r.kept.at[t], r.save_sem.at[buffer])

    def fetch(t):
        buffer = lax.rem(t, 2)
        return pltpu.make_async_copy(r.kept.at[t], r.counts.at[buffer], r.fetch_sem.at[buffer])

    def pool_chunk(p, c):
        t = p * chunks + c

        @pl.when(t >= 2)
        def _():
            save(t - 2).wait()

        buffer = lax.rem(t, 2)
        for i in range(CHUNK):
            source = lax.rem(node + c * at_once + i // groups, n_node)
            group = source * per_node + p * groups + i % groups
            put_counts(r.counts, buffer, i * BAG_GROUP, count_group(r.key, r.low, r.iota, group))
        save(t).start()
        sums = dot(r.counts[buffer], r.table[...]).astype(BF)
        for i in range(at_once):
            r.pooled[p, c * at_once + i] = sums[i * small : (i + 1) * small]

    def send_chunk(p, c):
        each((c + 1) * at_once, lambda k: out_node(p, k).start(), jnp.maximum(c * at_once, 1))

    def pack_piece(p):
        each(n_node, lambda k: out_node(p, k).wait_recv(), 1)
        arrived[p][node] = r.pooled[p, 0]

        def send(d):
            target = lax.rem(lane + d, n_local)
            for c in range(cap):
                r.packed[p, d, c] = arrived[p][r.pick[target * cap + c]]
            out_lane(p, d).start()

        each(n_local, send, 1)
        for c in range(cap):
            landed[p][lane * cap + c] = arrived[p][r.pick[lane * cap + c]]

    def unpack_piece(p):
        each(n_local, lambda d: out_lane(p, d).wait_recv(), 1)
        for q in range(n_node):
            r.x[p * small : (p + 1) * small, q * 128 : (q + 1) * 128] = landed[p][r.slot[q]]

    def send_parts(w, h, part):
        def columns(n):
            here = pl.ds(pl.multiple_of(n * 256, 256), 256)
            piece = part(here).astype(BF)
            for t in range(n_local):
                r.rank_send[w, h, t, :, here] = piece[t * share : (t + 1) * share]

        each(r.rank.shape[4] // 256, columns)
        each(n_local, lambda d: part_to(w, h, d).start(), 1)

    def reduce_parts(w, h):
        r.rank_recv[w, h, lane] = r.rank_send[w, h, lane]
        each(n_local, lambda d: part_to(w, h, d).wait_recv(), 1)
        summed = r.rank_recv[w, h, 0].astype(F32)
        for t in range(1, n_local):
            summed = summed + r.rank_recv[w, h, t].astype(F32)
        r.rank[w, h, lane] = summed.astype(BF)
        each(n_local, lambda d: share_to(w, h, d).start(), 1)

    def whole_rank(w, h):
        return r.rank[w, h].reshape(half, r.rank.shape[4])

    def side_by_side(ref, h):
        return jnp.concatenate([ref[q, rows(h), :] for q in range(n_node)], 1)

    def low_parts(h):
        send_parts(0, h, lambda here: dot(r.x[rows(h), :], r.down[:, here]))

    def cross(h):
        each(n_local, lambda d: share_to(0, h, d).wait_recv(), 1)

        def columns(n):
            here = pl.ds(pl.multiple_of(n * 512, 512), 512)
            added = dot(whole_rank(0, h), r.up[:, here]) + r.bias[:, here]
            x = r.x[rows(h), here].astype(F32)
            result = (x * added + x).astype(BF)
            r.term[rows(h), here] = added
            for i in range(4):
                r.crossed[n * 4 + i, rows(h), :] = result[:, i * 128 : (i + 1) * 128]

        each(total // 512, columns)

    def pre(h):
        def part(t):
            return dot(side_by_side(r.crossed, h), r.weight[:, pl.ds(pl.multiple_of(t * width, width), width)])

        def other_core(y):
            r.sib_send[h, y] = part(y * 2 + 1 - core).astype(BF)
            to_sibling(h, y).start()

        def my_core(i):
            dy = lax.rem(i + 1, chips)
            y = lax.rem(chip + dy, chips)
            mine = part(y * 2 + core)
            to_sibling(h, y).wait_recv()
            mine = mine + r.sib_recv[h, y].astype(F32)

            @pl.when(dy == 0)
            def _():
                r.pre_own[h] = mine

            @pl.when(dy > 0)
            def _():
                r.pre_send[h, dy] = mine.astype(BF)
                pre_to(h, dy).start()

        each(chips, other_core)
        each(chips, my_core)

    def activate(h):
        value = r.pre_own[h] + r.hbias[:, pl.ds(pl.multiple_of(lane * width, width), width)]
        for dy in range(1, chips):
            pre_to(h, dy).wait_recv()
            value = value + r.pre_recv[h, dy].astype(F32)
        sig = jax.nn.sigmoid(value)
        r.hidden[rows(h), :] = (value * sig).astype(BF)
        r.gpre[h, lane] = (r.hgrad[rows(h), :].astype(F32) * sig * (1.0 + value * (1.0 - sig))).astype(BF)
        each(chips, lambda dy: gpre_to(h, dy).start(), 1)
        forward(h, 0).start()

    def pass_on(h):
        def one(dy):
            gpre_to(h, dy).wait_recv()
            forward(h, dy).start()

        each(chips, one, 1)

    def back_chips(h, steps):
        sides = []
        for dy in steps:
            forward(h, dy).wait_recv()
            y = lax.rem(chip + chips - dy, chips)
            wide = pl.ds(pl.multiple_of(y * 2 * width, 2 * width), 2 * width)
            sides.append((y, wide))

        def columns(n):
            here = pl.ds(pl.multiple_of(n * 512, 512), 512)
            added = None
            for y, wide in sides:
                grads = jnp.concatenate([r.gpre[h, y * 2], r.gpre[h, y * 2 + 1]], 1)
                term = dot(grads, r.weight[here, wide], ((1,), (1,)))
                added = term if added is None else added + term
            if 0 in steps:
                r.gcross[rows(h), here] = added
            else:
                r.gcross[rows(h), here] += added

        each(total // 512, columns)

    def rank_grad(h):
        for q in range(n_node):
            here = slice(q * 128, (q + 1) * 128)
            r.gx[q, rows(h), :] = (r.gcross[rows(h), here] * r.x[rows(h), here].astype(F32)).astype(BF)
        send_parts(1, h, lambda here: dot(side_by_side(r.gx, h), r.up[here, :], ((1,), (1,))))

    def input_grad(h):
        each(n_local, lambda d: share_to(1, h, d).wait_recv(), 1)

        def columns(n):
            here = pl.ds(pl.multiple_of(n * 512, 512), 512)
            grads = r.gcross[rows(h), here]
            result = grads * r.term[rows(h), here] + grads + dot(whole_rank(1, h), r.down[here, :], ((1,), (1,)))
            result = result.astype(BF)
            for i in range(4):
                r.gx[n * 4 + i, rows(h), :] = result[:, i * 128 : (i + 1) * 128]

        each(total // 512, columns)

    def pack_back(p):
        here = slice(p * small, (p + 1) * small)
        each(n_local, lambda d: out_lane(p, d).wait_send(), 1)

        def send(d):
            target = lax.rem(lane + d, n_local)
            for c in range(cap):
                r.packed[p, d, c] = r.gx[r.back_pick[target * cap + c], here]
            back_lane(p, d).start()

        each(n_local, send, 1)
        for c in range(cap):
            returned[p][lane * cap + c] = r.gx[r.back_pick[lane * cap + c], here]

    def route_piece(p):
        each(n_node, lambda k: out_node(p, k).wait_send(), 1)
        each(n_local, lambda d: back_lane(p, d).wait_recv(), 1)

        def send(k):
            r.pooled[p, k] = returned[p][r.back_slot[lax.rem(node + k, n_node)]]
            back_node(p, k).start()

        each(n_node, send, 1)
        r.home[p, node] = returned[p][r.back_slot[node]]

    def add_piece(p):
        each(n_node, lambda k: back_node(p, k).wait_recv(), 1)

        def one_chunk(c):
            t = p * chunks + c
            buffer = lax.rem(t, 2)
            for i in range(at_once * small // 128):
                parts = [
                    r.home[p, lax.rem(node + c * at_once + i * (128 // small) + j, n_node)] for j in range(128 // small)
                ]
                r.home_t[:, i * 128 : (i + 1) * 128] = jnp.concatenate(parts, 0).T
            fetch(t).wait()
            for n in range(r.sums.shape[1] // 512):
                here = slice(n * 512, (n + 1) * 512)
                r.sums[:, here] += dot(r.home_t[...], r.counts[buffer, :, here])

            @pl.when(t + 2 < PIECES * chunks)
            def _():
                fetch(t + 2).start()

        each(chunks, one_chunk)

    my_columns = pl.ds(pl.multiple_of(lane * width, width), width)
    loads = [
        pltpu.make_async_copy(r.down_hbm, r.down, r.load_sem.at[0]),
        pltpu.make_async_copy(r.up_hbm, r.up, r.load_sem.at[1]),
        pltpu.make_async_copy(r.weight_hbm, r.weight, r.load_sem.at[2]),
        pltpu.make_async_copy(r.grad_hbm.at[:, my_columns], r.hgrad, r.load_sem.at[3]),
    ]
    barrier = greet(n_node, n_local, node, lane)
    fill = [
        pltpu.make_async_copy(r.idx_hbm, r.idx, r.load_sem.at[4]),
        pltpu.make_async_copy(r.size_hbm, r.size, r.load_sem.at[5]),
        pltpu.make_async_copy(r.table_hbm, r.table, r.load_sem.at[6]),
    ]
    for load in fill:
        load.start()
    for load in fill:
        load.wait()
    for load in loads:
        load.start()
    flatten_picks(r.idx, r.size, r.iota, r.key, r.low)
    each(chunks, lambda c: pool_chunk(0, c))
    pl.semaphore_wait(barrier, n_node + n_local - 2)
    for c in range(chunks):
        send_chunk(0, c)

    def turn(p):
        def one_chunk(c):
            pool_chunk(p, c)
            for piece in range(1, PIECES):

                @pl.when(p == piece)
                def _():
                    send_chunk(piece, c)

        each(chunks, one_chunk)
        for piece in range(PIECES - LAG):

            @pl.when(p == piece + LAG)
            def _():
                pack_piece(piece)

    each(PIECES, turn, 1)
    r.sums[...] = jnp.zeros_like(r.sums)
    for t in range(2):
        save(PIECES * chunks - 2 + t).wait()
    for t in range(2):
        fetch(t).start()
    for load in loads:
        load.wait()
    unpack_piece(2)
    unpack_piece(1)
    unpack_piece(0)
    unpack_piece(3)
    low_parts(0)
    pack_piece(5)
    reduce_parts(0, 0)
    pack_piece(7)
    cross(0)
    pre(0)
    unpack_piece(5)
    pack_piece(6)
    unpack_piece(4)
    activate(0)
    unpack_piece(6)
    unpack_piece(7)
    low_parts(1)
    back_chips(0, [0])
    pass_on(0)
    reduce_parts(0, 1)
    back_chips(0, [1, 2, 3])
    rank_grad(0)
    cross(1)
    pre(1)
    reduce_parts(1, 0)
    activate(1)
    back_chips(1, [0])
    input_grad(0)
    pack_back(0)
    pack_back(1)
    pass_on(1)
    back_chips(1, [1, 2, 3])
    rank_grad(1)
    pack_back(2)
    route_piece(0)
    reduce_parts(1, 1)
    pack_back(3)
    route_piece(2)
    route_piece(1)
    input_grad(1)
    pack_back(4)
    route_piece(3)
    pack_back(5)
    pack_back(6)
    add_piece(0)
    route_piece(4)
    add_piece(1)
    pack_back(7)
    route_piece(5)
    route_piece(6)
    add_piece(2)
    route_piece(7)
    add_piece(3)
    add_piece(4)
    add_piece(5)
    add_piece(6)
    add_piece(7)
    for n in range(r.sums.shape[1] // 128):
        r.table_grad[n * 128 : (n + 1) * 128, :] = r.sums[:, n * 128 : (n + 1) * 128].T

    for p in range(PIECES):
        each(n_node, lambda k: back_node(p, k).wait_send(), 1)
        each(n_local, lambda d: back_lane(p, d).wait_send(), 1)
    for h in range(HALVES):
        for w in range(2):
            each(n_local, lambda d: part_to(w, h, d).wait_send(), 1)
            each(n_local, lambda d: share_to(w, h, d).wait_send(), 1)
        each(chips, lambda y: to_sibling(h, y).wait_send())
        each(chips, lambda dy: pre_to(h, dy).wait_send(), 1)
        each(chips, lambda dy: gpre_to(h, dy).wait_send(), 1)
        each(chips, lambda dy: forward(h, dy).wait_send())


SMEM = pl.BlockSpec(memory_space=pltpu.SMEM)
VMEM = pl.BlockSpec(memory_space=pltpu.VMEM)
ANY = pl.BlockSpec(memory_space=pl.ANY)
SEM = pltpu.SemaphoreType.DMA


def train_step(operands, features, samples, n_node, n_local, cap):
    depth, hidden = operands["down_hbm"].shape[1], operands["weight_hbm"].shape[1]
    total = operands["down_hbm"].shape[0]
    table_rows, emb = operands["table_hbm"].shape
    groups = operands["idx_hbm"].shape[1] // BAG_GROUP
    small, half, width, chips = samples // PIECES, samples // HALVES, hidden // n_local, n_local // 2
    kept = (groups // CHUNK, CHUNK * BAG_GROUP, table_rows)
    outs = {
        "crossed": (jax.ShapeDtypeStruct((features, samples, emb), BF), VMEM),
        "hidden": (jax.ShapeDtypeStruct((samples, width), BF), VMEM),
        "table_grad": (jax.ShapeDtypeStruct((table_rows, emb), F32), VMEM),
        "kept": (jax.ShapeDtypeStruct(kept, BF), ANY),
    }
    parts = pltpu.VMEM((2, HALVES, n_local, half // n_local, depth), BF)
    quarter = pltpu.VMEM((HALVES, chips, half, width), BF)
    scratch = {
        "idx": pltpu.VMEM(operands["idx_hbm"].shape, jnp.int32),
        "size": pltpu.VMEM(operands["size_hbm"].shape, jnp.int32),
        "table": pltpu.VMEM((table_rows, emb), BF),
        "iota": pltpu.VMEM((LOW, LOW), BF),
        "key": pltpu.VMEM((groups, LOW), F32),
        "low": pltpu.VMEM((groups, LOW), F32),
        "counts": pltpu.VMEM((2, *kept[1:]), BF),
        "pooled": pltpu.VMEM((PIECES, n_node, small, emb), BF),
        "packed": pltpu.VMEM((PIECES, n_local, cap, small, emb), BF),
        "home": pltpu.VMEM((PIECES, n_node, small, emb), BF),
        "home_t": pltpu.VMEM((emb, kept[1]), BF),
        "sums": pltpu.VMEM((emb, table_rows), F32),
        "x": pltpu.VMEM((samples, total), BF),
        "down": pltpu.VMEM((total, depth), BF),
        "up": pltpu.VMEM((depth, total), BF),
        "weight": pltpu.VMEM((total, hidden), BF),
        "hgrad": pltpu.VMEM((samples, width), BF),
        "term": pltpu.VMEM((samples, total), F32),
        "gcross": pltpu.VMEM((samples, total), F32),
        "gx": pltpu.VMEM((features, samples, emb), BF),
        "rank_send": parts,
        "rank_recv": parts,
        "rank": parts,
        "sib_send": quarter,
        "sib_recv": quarter,
        "pre_send": quarter,
        "pre_recv": quarter,
        "pre_own": pltpu.VMEM((HALVES, half, width), F32),
        "gpre": pltpu.VMEM((HALVES, n_local, half, width), BF),
        "load_sem": SEM((7,)),
        "save_sem": SEM((2,)),
        "fetch_sem": SEM((2,)),
    }
    for p in range(PIECES):
        scratch[f"arrived{p}"] = pltpu.VMEM((n_node, small, emb), BF)
        scratch[f"landed{p}"] = pltpu.VMEM((n_local * cap, small, emb), BF)
        scratch[f"returned{p}"] = pltpu.VMEM((n_local * cap, small, emb), BF)
    for names, shape in (
        (("on", "bn"), (PIECES, n_node)),
        (("ol", "bl"), (PIECES, n_local)),
        (("rk", "sh"), (2, HALVES, n_local)),
        (("sb", "pr", "gp", "fw"), (HALVES, chips)),
    ):
        for name in names:
            scratch[name + "_s"] = SEM(shape)
            scratch[name + "_r"] = SEM(shape)
    places = {"pick": SMEM, "slot": SMEM, "back_pick": SMEM, "back_slot": SMEM}
    specs = [places.get(name, ANY if name.endswith("_hbm") else VMEM) for name in operands]
    names = [*operands, *outs, *scratch]
    return pl.pallas_call(
        functools.partial(step_kernel, names, n_node, n_local),
        out_shape=[shape for shape, _ in outs.values()],
        in_specs=specs,
        out_specs=[spec for _, spec in outs.values()],
        scratch_shapes=list(scratch.values()),
        compiler_params=pltpu.CompilerParams(collective_id=0, has_side_effects=True, vmem_limit_bytes=VMEM_LIMIT),
        name="train_step",
    )(*operands.values())


def on_device(
    owner_map,
    bag_sizes,
    indices,
    tables,
    cross_down,
    cross_up,
    cross_bias,
    mlp_weight,
    mlp_bias,
    hidden_grad,
):
    node_count = lax.axis_size("node")
    lane_count = lax.axis_size("local")
    my_lane = lax.axis_index("local")
    capacity = node_count // lane_count + 1
    slot_total = lane_count * capacity
    samples = hidden_grad.shape[0]
    hidden_width = hidden_grad.shape[1]
    feat_ids = jnp.arange(owner_map.shape[0], dtype=jnp.int32)
    node_ids = jnp.arange(node_count, dtype=jnp.int32)
    source_dev = node_ids * lane_count + my_lane
    source_feat = jnp.sum(
        jnp.where(owner_map[None, :] == source_dev[:, None], feat_ids[None, :], 0), axis=1
    )
    source_group = source_feat // node_count
    same_group = source_group[:, None] == source_group[None, :]
    earlier = node_ids[None, :] < node_ids[:, None]
    source_slot = source_group * capacity + jnp.sum(
        (same_group & earlier).astype(jnp.int32), axis=1
    )
    group_owners = lax.dynamic_slice_in_dim(owner_map, my_lane * node_count, node_count)
    owner_lane = group_owners % lane_count
    owner_node = group_owners // lane_count
    ahead_same = (owner_lane[:, None] == owner_lane[None, :]) & (
        owner_node[None, :] < owner_node[:, None]
    )
    owner_slot = owner_lane * capacity + jnp.sum(ahead_same.astype(jnp.int32), axis=1)
    slot_ids = jnp.arange(slot_total, dtype=jnp.int32)
    pick_source = jnp.sum(
        jnp.where(source_slot[None, :] == slot_ids[:, None], node_ids[None, :], 0), axis=1
    )
    back_source = jnp.sum(
        jnp.where(owner_slot[None, :] == slot_ids[:, None], node_ids[None, :], 0), axis=1
    )

    operands = {
        "pick": pick_source,
        "slot": owner_slot,
        "back_pick": back_source,
        "back_slot": source_slot,
        "idx_hbm": indices[0].T,
        "size_hbm": bag_sizes,
        "table_hbm": tables,
        "bias": cross_bias.reshape(1, -1),
        "hbias": mlp_bias.reshape(1, -1),
        "grad_hbm": hidden_grad,
        "down_hbm": cross_down.reshape(-1, cross_down.shape[2]),
        "up_hbm": cross_up.reshape(cross_up.shape[0], -1),
        "weight_hbm": mlp_weight.reshape(-1, hidden_width),
    }
    crossed, hidden, table_grad, _ = train_step(operands, node_count, samples, node_count, lane_count, capacity)
    return (crossed, hidden, table_grad)


def solution(mesh):
    return jax.shard_map(
        on_device,
        mesh=mesh,
        in_specs=(
            P(),
            P(("node", "local"), None),
            P(("node", "local"), None, None),
            P(("node", "local"), None),
            P("local", None, None),
            P(None, "local", None),
            P("local", None),
            P("local", None, None),
            P(),
            P("node", None),
        ),
        out_specs=(P("local", "node", None), P("node", "local"), P(("node", "local"), None)),
        check_vma=False,
    )
```

```python
import functools
import types

import jax
import jax.numpy as jnp
from jax import lax
from jax.experimental import pallas as pl
from jax.experimental.pallas import tpu as pltpu
from jax.sharding import PartitionSpec as P

BF = jnp.bfloat16
F32 = jnp.float32
MESH = pl.DeviceIdType.MESH
PIECES = 8
HALVES = 2
CHUNK = 16
LAG = 2
VMEM_LIMIT = 62 << 20
BAG_GROUP = 32
LOW = 256


def dot(a, b, contract=((1,), (0,))):
    return lax.dot_general(a, b, (contract, ((), ())), preferred_element_type=F32)


def greet(n_node, n_local, node, lane):
    barrier = pltpu.get_barrier_semaphore()

    def by_node(k, carry):
        peer = lax.rem(node + k, n_node)
        pl.semaphore_signal(barrier, inc=1, device_id=(peer, lane), device_id_type=MESH)
        return carry

    def by_lane(d, carry):
        peer = lax.rem(lane + d, n_local)
        pl.semaphore_signal(barrier, inc=1, device_id=(node, peer), device_id_type=MESH)
        return carry

    lax.fori_loop(1, n_node, by_node, 0)
    lax.fori_loop(1, n_local, by_lane, 0)
    return barrier


def flatten_picks(idx_ref, size_ref, iota_ref, key_ref, low_ref):
    iota_ref[...] = lax.broadcasted_iota(jnp.int32, iota_ref.shape, 0).astype(F32).astype(BF)
    lanes = lax.broadcasted_iota(jnp.int32, (1, 128), 1)
    depth = lax.broadcasted_iota(jnp.int32, (8, 128), 0)

    def eight_groups(b, carry):
        rows = [[], []]
        for half in range(2):
            off = pl.multiple_of(b * 256 + half * 128, 128)
            picks = jnp.where(depth < size_ref[:, pl.ds(off, 128)], idx_ref[:, pl.ds(off, 128)], -1)
            turned = [picks] + [pltpu.roll(picks, 32 * d, 1) for d in (1, 2, 3)]
            for group in range(4):
                for h in range(2):
                    row = turned[(3 - group) % 4][4 * h + 3 : 4 * h + 4]
                    for q in (2, 1, 0):
                        source = turned[(q - group) % 4][4 * h + q : 4 * h + q + 1]
                        row = jnp.where(lanes < 32 * (q + 1), source, row)
                    rows[h].append(row)
        here = pl.ds(pl.multiple_of(b * 8, 8), 8)
        for h in range(2):
            picks = jnp.concatenate(rows[h], 0)
            key_ref[here, h * 128 : (h + 1) * 128] = ((picks >> 8) * 32 + (lanes & 31)).astype(F32)
            low_ref[here, h * 128 : (h + 1) * 128] = (picks & 255).astype(F32)
        return carry

    lax.fori_loop(0, idx_ref.shape[1] // 256, eight_groups, 0)


def count_group(key_ref, low_ref, iota_ref, group):
    iota = iota_ref[...]
    one, zero = jnp.ones((), BF), jnp.zeros((), BF)
    hot = []
    for ref in (key_ref, low_ref):
        row = jnp.broadcast_to(ref[pl.ds(group, 1), :], (16, LOW)).astype(BF)
        hot.append(jnp.where(jnp.concatenate([row] * 16, 0) == iota, one, zero))
    return dot(hot[0], hot[1], ((1,), (1,))).astype(BF)


def put_counts(count_ref, where, row, counts):
    for h in range(8):
        count_ref[where, pl.ds(row, BAG_GROUP), h * LOW : (h + 1) * LOW] = counts[h * 32 : (h + 1) * 32]


def step_kernel(names, n_node, n_local, *refs):
    r = types.SimpleNamespace(**dict(zip(names, refs)))
    node, lane = lax.axis_index("node"), lax.axis_index("local")
    chips = n_local // 2
    chip, core = lane // 2, lax.rem(lane, 2)
    sibling = chip * 2 + 1 - core
    cap, small = r.packed.shape[2], r.packed.shape[3]
    samples, total = r.x.shape
    half = samples // HALVES
    share = half // n_local
    width = r.gpre.shape[3]
    per_node = samples // BAG_GROUP
    groups = small // BAG_GROUP
    at_once = CHUNK // groups
    chunks = n_node // at_once
    arrived = [getattr(r, f"arrived{p}") for p in range(PIECES)]
    landed = [getattr(r, f"landed{p}") for p in range(PIECES)]
    returned = [getattr(r, f"returned{p}") for p in range(PIECES)]

    def rows(h):
        return slice(h * half, (h + 1) * half)

    def each(count, act, first=0):
        def body(i, carry):
            act(i)
            return carry

        lax.fori_loop(first, count, body, 0)

    def remote(src, dst, sems, at, peer):
        send, recv = sems
        return pltpu.make_async_remote_copy(
            src_ref=src, dst_ref=dst, send_sem=send.at[at], recv_sem=recv.at[at], device_id=peer, device_id_type=MESH
        )

    def node_peer(k):
        return lax.rem(node + k, n_node), lane

    def lane_peer(d):
        return node, lax.rem(lane + d, n_local)

    def chip_peer(dy):
        return node, lax.rem(chip + dy, chips) * 2 + core

    def find_slots():
        features = r.owner.shape[1]
        wide = (features, features)
        here = jnp.broadcast_to(r.owner[...].astype(F32), wide)
        owner, other = here.T.astype(jnp.int32), here.astype(jnp.int32)
        feature, at = lax.broadcasted_iota(jnp.int32, wide, 0), lax.broadcasted_iota(jnp.int32, wide, 1)
        group, other_group = feature // n_node, at // n_node
        own_lane, own_node = lax.rem(owner, n_local), owner // n_local
        ahead = (at < feature) & (group == other_group) & (lax.rem(other, n_local) == own_lane)
        rank = jnp.sum(ahead.astype(F32), axis=1, keepdims=True).astype(jnp.int32)
        source_slot, target_slot = group * cap + rank, own_lane * cap + rank

        def put(row, where, value, limit):
            chosen = jnp.where(where, value, 0).astype(F32)
            found = jnp.sum(chosen, axis=0, keepdims=True).astype(jnp.int32)
            r.slots_v[row : row + 1, :] = jnp.clip(found, 0, limit - 1)

        put(0, (own_lane == lane) & (source_slot == at), own_node, n_node)
        put(1, feature == lane * n_node + at, target_slot, n_local * cap)
        put(2, (group == lane) & (target_slot == at), feature - lane * n_node, n_node)
        put(3, owner == at * n_local + lane, source_slot, n_local * cap)
        copy = pltpu.make_async_copy(r.slots_v, r.slots, r.load_sem.at[7])
        copy.start()
        copy.wait()

    def out_node(p, k):
        return remote(r.pooled.at[p, k], arrived[p].at[node], (r.on_s, r.on_r), (p, k), node_peer(k))

    def out_lane(p, d):
        here = pl.ds(lane * cap, cap)
        return remote(r.packed.at[p, d], landed[p].at[here], (r.ol_s, r.ol_r), (p, d), lane_peer(d))

    def back_lane(p, d):
        here = pl.ds(lane * cap, cap)
        return remote(r.packed.at[p, d], returned[p].at[here], (r.bl_s, r.bl_r), (p, d), lane_peer(d))

    def back_node(p, k):
        return remote(r.pooled.at[p, k], r.home.at[p, node], (r.bn_s, r.bn_r), (p, k), node_peer(k))

    def part_to(w, h, d):
        peer = lane_peer(d)
        return remote(r.rank_send.at[w, h, peer[1]], r.rank_recv.at[w, h, lane], (r.rk_s, r.rk_r), (w, h, d), peer)

    def share_to(w, h, d):
        return remote(r.rank.at[w, h, lane], r.rank.at[w, h, lane], (r.sh_s, r.sh_r), (w, h, d), lane_peer(d))

    def to_sibling(h, y):
        return remote(r.sib_send.at[h, y], r.sib_recv.at[h, y], (r.sb_s, r.sb_r), (h, y), (node, sibling))

    def pre_to(h, dy):
        return remote(r.pre_send.at[h, dy], r.pre_recv.at[h, dy], (r.pr_s, r.pr_r), (h, dy), chip_peer(dy))

    def gpre_to(h, dy):
        return remote(r.gpre.at[h, lane], r.gpre.at[h, lane], (r.gp_s, r.gp_r), (h, dy), chip_peer(dy))

    def forward(h, dy):
        source = lax.rem(chip + chips - dy, chips) * 2 + core
        return remote(r.gpre.at[h, source], r.gpre.at[h, source], (r.fw_s, r.fw_r), (h, dy), (node, sibling))

    def save(t):
        buffer = lax.rem(t, 2)
        return pltpu.make_async_copy(r.counts.at[buffer], r.kept.at[t], r.save_sem.at[buffer])

    def fetch(t):
        buffer = lax.rem(t, 2)
        return pltpu.make_async_copy(r.kept.at[t], r.counts.at[buffer], r.fetch_sem.at[buffer])

    def pool_chunk(p, c):
        t = p * chunks + c

        @pl.when(t >= 2)
        def _():
            save(t - 2).wait()

        buffer = lax.rem(t, 2)
        for i in range(CHUNK):
            source = lax.rem(node + c * at_once + i // groups, n_node)
            group = source * per_node + p * groups + i % groups
            put_counts(r.counts, buffer, i * BAG_GROUP, count_group(r.key, r.low, r.iota, group))
        save(t).start()
        sums = dot(r.counts[buffer], r.table[...]).astype(BF)
        for i in range(at_once):
            r.pooled[p, c * at_once + i] = sums[i * small : (i + 1) * small]

    def send_chunk(p, c):
        each((c + 1) * at_once, lambda k: out_node(p, k).start(), jnp.maximum(c * at_once, 1))

    def pack_piece(p):
        each(n_node, lambda k: out_node(p, k).wait_recv(), 1)
        arrived[p][node] = r.pooled[p, 0]

        def send(d):
            target = lax.rem(lane + d, n_local)
            for c in range(cap):
                r.packed[p, d, c] = arrived[p][r.slots[0, target * cap + c]]
            out_lane(p, d).start()

        each(n_local, send, 1)
        for c in range(cap):
            landed[p][lane * cap + c] = arrived[p][r.slots[0, lane * cap + c]]

    def unpack_piece(p):
        each(n_local, lambda d: out_lane(p, d).wait_recv(), 1)
        for q in range(n_node):
            r.x[p * small : (p + 1) * small, q * 128 : (q + 1) * 128] = landed[p][r.slots[1, q]]

    def lay_up():
        depth = r.up.shape[0] // r.gx.shape[0]

        def block(i):
            turned = jnp.swapaxes(r.gx[i].reshape(depth, n_node, 128), 0, 1)
            for q in range(n_node):
                r.up[pl.ds(pl.multiple_of(i * depth, depth), depth), q * 128 : (q + 1) * 128] = turned[q]

        each(r.gx.shape[0], block)

    def send_parts(w, h, part):
        def columns(n):
            here = pl.ds(pl.multiple_of(n * 256, 256), 256)
            piece = part(here).astype(BF)
            for t in range(n_local):
                r.rank_send[w, h, t, :, here] = piece[t * share : (t + 1) * share]

        each(r.rank.shape[4] // 256, columns)
        each(n_local, lambda d: part_to(w, h, d).start(), 1)

    def reduce_parts(w, h):
        r.rank_recv[w, h, lane] = r.rank_send[w, h, lane]
        each(n_local, lambda d: part_to(w, h, d).wait_recv(), 1)
        summed = r.rank_recv[w, h, 0].astype(F32)
        for t in range(1, n_local):
            summed = summed + r.rank_recv[w, h, t].astype(F32)
        r.rank[w, h, lane] = summed.astype(BF)
        each(n_local, lambda d: share_to(w, h, d).start(), 1)

    def whole_rank(w, h):
        return r.rank[w, h].reshape(half, r.rank.shape[4])

    def side_by_side(ref, h):
        return jnp.concatenate([ref[q, rows(h), :] for q in range(n_node)], 1)

    def low_parts(h):
        send_parts(0, h, lambda here: dot(r.x[rows(h), :], r.down[:, here]))

    def cross(h):
        each(n_local, lambda d: share_to(0, h, d).wait_recv(), 1)

        def columns(n):
            here = pl.ds(pl.multiple_of(n * 512, 512), 512)
            added = dot(whole_rank(0, h), r.up[:, here]) + r.bias[:, here]
            x = r.x[rows(h), here].astype(F32)
            result = (x * added + x).astype(BF)
            r.term[rows(h), here] = added
            for i in range(4):
                r.crossed[n * 4 + i, rows(h), :] = result[:, i * 128 : (i + 1) * 128]

        each(total // 512, columns)
        keep_crossed(h).start()

    def keep_crossed(h):
        return pltpu.make_async_copy(r.crossed.at[:, rows(h)], r.crossed_out.at[:, rows(h)], r.out_sem.at[h])

    def pre(h):
        def part(t):
            return dot(side_by_side(r.crossed, h), r.weight[:, pl.ds(pl.multiple_of(t * width, width), width)])

        def other_core(y):
            r.sib_send[h, y] = part(y * 2 + 1 - core).astype(BF)
            to_sibling(h, y).start()

        def my_core(i):
            dy = lax.rem(i + 1, chips)
            y = lax.rem(chip + dy, chips)
            mine = part(y * 2 + core)
            to_sibling(h, y).wait_recv()
            mine = mine + r.sib_recv[h, y].astype(F32)

            @pl.when(dy == 0)
            def _():
                r.pre_own[h] = mine

            @pl.when(dy > 0)
            def _():
                r.pre_send[h, dy] = mine.astype(BF)
                pre_to(h, dy).start()

        each(chips, other_core)
        each(chips, my_core)

    def activate(h):
        value = r.pre_own[h] + r.hbias[:, pl.ds(pl.multiple_of(lane * width, width), width)]
        for dy in range(1, chips):
            pre_to(h, dy).wait_recv()
            value = value + r.pre_recv[h, dy].astype(F32)
        sig = jax.nn.sigmoid(value)
        r.hidden[rows(h), :] = (value * sig).astype(BF)
        r.gpre[h, lane] = (r.hgrad[rows(h), :].astype(F32) * sig * (1.0 + value * (1.0 - sig))).astype(BF)
        each(chips, lambda dy: gpre_to(h, dy).start(), 1)
        forward(h, 0).start()

    def pass_on(h):
        def one(dy):
            gpre_to(h, dy).wait_recv()
            forward(h, dy).start()

        each(chips, one, 1)

    def back_chips(h, steps):
        sides = []
        for dy in steps:
            forward(h, dy).wait_recv()
            y = lax.rem(chip + chips - dy, chips)
            wide = pl.ds(pl.multiple_of(y * 2 * width, 2 * width), 2 * width)
            sides.append((y, wide))

        def columns(n):
            here = pl.ds(pl.multiple_of(n * 512, 512), 512)
            added = None
            for y, wide in sides:
                grads = jnp.concatenate([r.gpre[h, y * 2], r.gpre[h, y * 2 + 1]], 1)
                term = dot(grads, r.weight[here, wide], ((1,), (1,)))
                added = term if added is None else added + term
            if 0 in steps:
                r.gcross[rows(h), here] = added
            else:
                r.gcross[rows(h), here] += added

        each(total // 512, columns)

    def rank_grad(h):
        for q in range(n_node):
            here = slice(q * 128, (q + 1) * 128)
            r.gx[q, rows(h), :] = (r.gcross[rows(h), here] * r.x[rows(h), here].astype(F32)).astype(BF)
        send_parts(1, h, lambda here: dot(side_by_side(r.gx, h), r.up[here, :], ((1,), (1,))))

    def input_grad(h):
        each(n_local, lambda d: share_to(1, h, d).wait_recv(), 1)

        def columns(n):
            here = pl.ds(pl.multiple_of(n * 512, 512), 512)
            grads = r.gcross[rows(h), here]
            result = grads * r.term[rows(h), here] + grads + dot(whole_rank(1, h), r.down[here, :], ((1,), (1,)))
            result = result.astype(BF)
            for i in range(4):
                r.gx[n * 4 + i, rows(h), :] = result[:, i * 128 : (i + 1) * 128]

        each(total // 512, columns)

    def pack_back(p):
        here = slice(p * small, (p + 1) * small)
        each(n_local, lambda d: out_lane(p, d).wait_send(), 1)

        def send(d):
            target = lax.rem(lane + d, n_local)
            for c in range(cap):
                r.packed[p, d, c] = r.gx[r.slots[2, target * cap + c], here]
            back_lane(p, d).start()

        each(n_local, send, 1)
        for c in range(cap):
            returned[p][lane * cap + c] = r.gx[r.slots[2, lane * cap + c], here]

    def route_piece(p):
        each(n_node, lambda k: out_node(p, k).wait_send(), 1)
        each(n_local, lambda d: back_lane(p, d).wait_recv(), 1)

        def send(k):
            r.pooled[p, k] = returned[p][r.slots[3, lax.rem(node + k, n_node)]]
            back_node(p, k).start()

        each(n_node, send, 1)
        r.home[p, node] = returned[p][r.slots[3, node]]

    def add_piece(p):
        each(n_node, lambda k: back_node(p, k).wait_recv(), 1)

        def one_chunk(c):
            t = p * chunks + c
            buffer = lax.rem(t, 2)
            for i in range(at_once * small // 128):
                parts = [
                    r.home[p, lax.rem(node + c * at_once + i * (128 // small) + j, n_node)] for j in range(128 // small)
                ]
                r.home_t[:, i * 128 : (i + 1) * 128] = jnp.concatenate(parts, 0).T
            fetch(t).wait()
            for n in range(r.sums.shape[1] // 512):
                here = slice(n * 512, (n + 1) * 512)
                r.sums[:, here] += dot(r.home_t[...], r.counts[buffer, :, here])

            @pl.when(t + 2 < PIECES * chunks)
            def _():
                fetch(t + 2).start()

        each(chunks, one_chunk)

    my_columns = pl.ds(pl.multiple_of(lane * width, width), width)
    loads = [
        pltpu.make_async_copy(r.down_hbm, r.down, r.load_sem.at[0]),
        pltpu.make_async_copy(r.up_hbm, r.gx, r.load_sem.at[1]),
        pltpu.make_async_copy(r.weight_hbm, r.weight, r.load_sem.at[2]),
        pltpu.make_async_copy(r.grad_hbm.at[:, my_columns], r.hgrad, r.load_sem.at[3]),
    ]
    barrier = greet(n_node, n_local, node, lane)
    fill = [
        pltpu.make_async_copy(r.idx_hbm, r.idx, r.load_sem.at[4]),
        pltpu.make_async_copy(r.size_hbm, r.size, r.load_sem.at[5]),
        pltpu.make_async_copy(r.table_hbm, r.table, r.load_sem.at[6]),
    ]
    for load in fill:
        load.start()
    r.slots_v[...] = jnp.zeros_like(r.slots_v)
    find_slots()
    for load in fill:
        load.wait()
    for load in loads:
        load.start()
    flatten_picks(r.idx, r.size, r.iota, r.key, r.low)
    each(chunks, lambda c: pool_chunk(0, c))
    pl.semaphore_wait(barrier, n_node + n_local - 2)
    for c in range(chunks):
        send_chunk(0, c)

    def turn(p):
        def one_chunk(c):
            pool_chunk(p, c)
            for piece in range(1, PIECES):

                @pl.when(p == piece)
                def _():
                    send_chunk(piece, c)

        each(chunks, one_chunk)
        for piece in range(PIECES - LAG):

            @pl.when(p == piece + LAG)
            def _():
                pack_piece(piece)

    each(PIECES, turn, 1)
    r.sums[...] = jnp.zeros_like(r.sums)
    for t in range(2):
        save(PIECES * chunks - 2 + t).wait()
    for t in range(2):
        fetch(t).start()
    for load in loads:
        load.wait()
    unpack_piece(0)
    unpack_piece(1)
    unpack_piece(3)
    unpack_piece(2)
    low_parts(0)
    pack_piece(6)
    unpack_piece(5)
    unpack_piece(4)
    lay_up()
    reduce_parts(0, 0)
    pack_piece(7)
    unpack_piece(6)
    cross(0)
    pre(0)
    unpack_piece(7)
    low_parts(1)
    activate(0)
    back_chips(0, [0])
    pass_on(0)
    reduce_parts(0, 1)
    back_chips(0, [1, 2, 3])
    rank_grad(0)
    cross(1)
    pre(1)
    reduce_parts(1, 0)
    activate(1)
    back_chips(1, [0])
    input_grad(0)
    pack_back(0)
    pack_back(1)
    pass_on(1)
    back_chips(1, [1, 2, 3])
    rank_grad(1)
    route_piece(0)
    pack_back(2)
    reduce_parts(1, 1)
    pack_back(3)
    route_piece(2)
    route_piece(1)
    input_grad(1)
    pack_back(4)
    route_piece(3)
    pack_back(5)
    route_piece(4)
    pack_back(6)
    add_piece(0)
    add_piece(1)
    pack_back(7)
    route_piece(5)
    route_piece(6)
    add_piece(2)
    route_piece(7)
    add_piece(3)
    add_piece(4)
    add_piece(5)
    add_piece(6)
    add_piece(7)
    for n in range(r.sums.shape[1] // 128):
        r.table_grad[n * 128 : (n + 1) * 128, :] = r.sums[:, n * 128 : (n + 1) * 128].T

    for p in range(PIECES):
        each(n_node, lambda k: back_node(p, k).wait_send(), 1)
        each(n_local, lambda d: back_lane(p, d).wait_send(), 1)
    for h in range(HALVES):
        keep_crossed(h).wait()
        for w in range(2):
            each(n_local, lambda d: part_to(w, h, d).wait_send(), 1)
            each(n_local, lambda d: share_to(w, h, d).wait_send(), 1)
        each(chips, lambda y: to_sibling(h, y).wait_send())
        each(chips, lambda dy: pre_to(h, dy).wait_send(), 1)
        each(chips, lambda dy: gpre_to(h, dy).wait_send(), 1)
        each(chips, lambda dy: forward(h, dy).wait_send())


VMEM = pl.BlockSpec(memory_space=pltpu.VMEM)
ANY = pl.BlockSpec(memory_space=pl.ANY)
SEM = pltpu.SemaphoreType.DMA


def train_step(operands, features, samples, n_node, n_local, cap):
    depth, hidden = operands["down_hbm"].shape[1], operands["weight_hbm"].shape[1]
    total = operands["down_hbm"].shape[0]
    table_rows, emb = operands["table_hbm"].shape
    groups = operands["idx_hbm"].shape[1] // BAG_GROUP
    small, half, width, chips = samples // PIECES, samples // HALVES, hidden // n_local, n_local // 2
    kept = (groups // CHUNK, CHUNK * BAG_GROUP, table_rows)
    outs = {
        "crossed_out": (jax.ShapeDtypeStruct((features, samples, emb), BF), ANY),
        "hidden": (jax.ShapeDtypeStruct((samples, width), BF), VMEM),
        "table_grad": (jax.ShapeDtypeStruct((table_rows, emb), F32), VMEM),
        "kept": (jax.ShapeDtypeStruct(kept, BF), ANY),
    }
    parts = pltpu.VMEM((2, HALVES, n_local, half // n_local, depth), BF)
    quarter = pltpu.VMEM((HALVES, chips, half, width), BF)
    scratch = {
        "idx": pltpu.VMEM(operands["idx_hbm"].shape, jnp.int32),
        "size": pltpu.VMEM(operands["size_hbm"].shape, jnp.int32),
        "table": pltpu.VMEM((table_rows, emb), BF),
        "slots_v": pltpu.VMEM((8, operands["owner"].shape[1]), jnp.int32),
        "slots": pltpu.SMEM((8, operands["owner"].shape[1]), jnp.int32),
        "iota": pltpu.VMEM((LOW, LOW), BF),
        "key": pltpu.VMEM((groups, LOW), F32),
        "low": pltpu.VMEM((groups, LOW), F32),
        "counts": pltpu.VMEM((2, *kept[1:]), BF),
        "pooled": pltpu.VMEM((PIECES, n_node, small, emb), BF),
        "packed": pltpu.VMEM((PIECES, n_local, cap, small, emb), BF),
        "home": pltpu.VMEM((PIECES, n_node, small, emb), BF),
        "home_t": pltpu.VMEM((emb, kept[1]), BF),
        "sums": pltpu.VMEM((emb, table_rows), F32),
        "x": pltpu.VMEM((samples, total), BF),
        "down": pltpu.VMEM((total, depth), BF),
        "up": pltpu.VMEM((depth, total), BF),
        "weight": pltpu.VMEM((total, hidden), BF),
        "hgrad": pltpu.VMEM((samples, width), BF),
        "term": pltpu.VMEM((samples, total), F32),
        "gcross": pltpu.VMEM((samples, total), F32),
        "gx": pltpu.VMEM((features, samples, emb), BF),
        "crossed": pltpu.VMEM((features, samples, emb), BF),
        "out_sem": SEM((HALVES,)),
        "rank_send": parts,
        "rank_recv": parts,
        "rank": parts,
        "sib_send": quarter,
        "sib_recv": quarter,
        "pre_send": quarter,
        "pre_recv": quarter,
        "pre_own": pltpu.VMEM((HALVES, half, width), F32),
        "gpre": pltpu.VMEM((HALVES, n_local, half, width), BF),
        "load_sem": SEM((8,)),
        "save_sem": SEM((2,)),
        "fetch_sem": SEM((2,)),
    }
    for p in range(PIECES):
        scratch[f"arrived{p}"] = pltpu.VMEM((n_node, small, emb), BF)
        scratch[f"landed{p}"] = pltpu.VMEM((n_local * cap, small, emb), BF)
        scratch[f"returned{p}"] = pltpu.VMEM((n_local * cap, small, emb), BF)
    for names, shape in (
        (("on", "bn"), (PIECES, n_node)),
        (("ol", "bl"), (PIECES, n_local)),
        (("rk", "sh"), (2, HALVES, n_local)),
        (("sb", "pr", "gp", "fw"), (HALVES, chips)),
    ):
        for name in names:
            scratch[name + "_s"] = SEM(shape)
            scratch[name + "_r"] = SEM(shape)
    specs = [ANY if name.endswith("_hbm") else VMEM for name in operands]
    names = [*operands, *outs, *scratch]
    return pl.pallas_call(
        functools.partial(step_kernel, names, n_node, n_local),
        out_shape=[shape for shape, _ in outs.values()],
        in_specs=specs,
        out_specs=[spec for _, spec in outs.values()],
        scratch_shapes=list(scratch.values()),
        compiler_params=pltpu.CompilerParams(collective_id=0, has_side_effects=True, vmem_limit_bytes=VMEM_LIMIT),
        name="train_step",
    )(*operands.values())


def hand_out_kernel(count, *refs):
    given, taken, held = refs[:count], refs[count : 2 * count], refs[2 * count : 3 * count]
    read_sem, write_sem = refs[3 * count :]
    reads, writes = [], []
    for source, target, middle in zip(given, taken, held):
        rows = source.shape[0] // 4
        for i in range(4):
            part, at = pl.ds(i * rows, rows), len(reads)
            reads.append(pltpu.make_async_copy(source.at[part], middle.at[part], read_sem.at[at]))
            writes.append(pltpu.make_async_copy(middle.at[part], target.at[part], write_sem.at[at]))
    for copy in reads:
        copy.start()
    for read, write in zip(reads, writes):
        read.wait()
        write.start()
    for copy in writes:
        copy.wait()


def hand_out(*arrays):
    count = len(arrays)
    return pl.pallas_call(
        functools.partial(hand_out_kernel, count),
        out_shape=[jax.ShapeDtypeStruct(a.shape, a.dtype) for a in arrays],
        in_specs=[ANY] * count,
        out_specs=[ANY] * count,
        scratch_shapes=[*[pltpu.VMEM(a.shape, a.dtype) for a in arrays], SEM((4 * count,)), SEM((4 * count,))],
        compiler_params=pltpu.CompilerParams(vmem_limit_bytes=16 << 20),
        name="hand_out",
    )(*arrays)


def on_device(
    owner_map,
    bag_sizes,
    indices,
    tables,
    cross_down,
    cross_up,
    cross_bias,
    mlp_weight,
    mlp_bias,
    hidden_grad,
):
    node_count = lax.axis_size("node")
    lane_count = lax.axis_size("local")
    capacity = node_count // lane_count + 1
    samples = hidden_grad.shape[0]
    hidden_width = hidden_grad.shape[1]
    operands = {
        "owner": owner_map.reshape(1, -1),
        "bias": cross_bias.reshape(1, -1),
        "hbias": mlp_bias.reshape(1, -1),
        "idx_hbm": indices[0].T,
        "size_hbm": bag_sizes,
        "table_hbm": tables,
        "grad_hbm": hidden_grad,
        "down_hbm": cross_down.reshape(-1, cross_down.shape[2]),
        "up_hbm": cross_up.reshape(node_count, -1, cross_up.shape[2]),
        "weight_hbm": mlp_weight.reshape(-1, hidden_width),
    }
    crossed, hidden, table_grad, _ = train_step(operands, node_count, samples, node_count, lane_count, capacity)
    return hand_out(crossed, hidden, table_grad)


def solution(mesh):
    return jax.shard_map(
        on_device,
        mesh=mesh,
        in_specs=(
            P(),
            P(("node", "local"), None),
            P(("node", "local"), None, None),
            P(("node", "local"), None),
            P("local", None, None),
            P(None, "local", None),
            P("local", None),
            P("local", None, None),
            P(),
            P("node", None),
        ),
        out_specs=(P("local", "node", None), P("node", "local"), P(("node", "local"), None)),
        check_vma=False,
    )
```

```python
import functools
import types

import jax
import jax.numpy as jnp
from jax import lax
from jax.experimental import pallas as pl
from jax.experimental.pallas import tpu as pltpu
from jax.sharding import PartitionSpec as P

BF = jnp.bfloat16
F32 = jnp.float32
MESH = pl.DeviceIdType.MESH
PIECES = 8
HALVES = 2
CHUNK = 16
LAG = 2
VMEM_LIMIT = 62 << 20
BAG_GROUP = 32
LOW = 256


def dot(a, b, contract=((1,), (0,))):
    return lax.dot_general(a, b, (contract, ((), ())), preferred_element_type=F32)


def greet(n_node, n_local, node, lane):
    barrier = pltpu.get_barrier_semaphore()

    def by_node(k, carry):
        peer = lax.rem(node + k, n_node)
        pl.semaphore_signal(barrier, inc=1, device_id=(peer, lane), device_id_type=MESH)
        return carry

    def by_lane(d, carry):
        peer = lax.rem(lane + d, n_local)
        pl.semaphore_signal(barrier, inc=1, device_id=(node, peer), device_id_type=MESH)
        return carry

    lax.fori_loop(1, n_node, by_node, 0)
    lax.fori_loop(1, n_local, by_lane, 0)
    return barrier


def flatten_picks(idx_ref, size_ref, iota_ref, key_ref, low_ref):
    iota_ref[...] = lax.broadcasted_iota(jnp.int32, iota_ref.shape, 0).astype(F32).astype(BF)
    lanes = lax.broadcasted_iota(jnp.int32, (1, 128), 1)
    depth = lax.broadcasted_iota(jnp.int32, (8, 128), 0)

    def eight_groups(b, carry):
        rows = [[], []]
        for half in range(2):
            off = pl.multiple_of(b * 256 + half * 128, 128)
            picks = jnp.where(depth < size_ref[:, pl.ds(off, 128)], idx_ref[:, pl.ds(off, 128)], -1)
            turned = [picks] + [pltpu.roll(picks, 32 * d, 1) for d in (1, 2, 3)]
            for group in range(4):
                for h in range(2):
                    row = turned[(3 - group) % 4][4 * h + 3 : 4 * h + 4]
                    for q in (2, 1, 0):
                        source = turned[(q - group) % 4][4 * h + q : 4 * h + q + 1]
                        row = jnp.where(lanes < 32 * (q + 1), source, row)
                    rows[h].append(row)
        here = pl.ds(pl.multiple_of(b * 8, 8), 8)
        for h in range(2):
            picks = jnp.concatenate(rows[h], 0)
            key_ref[here, h * 128 : (h + 1) * 128] = ((picks >> 8) * 32 + (lanes & 31)).astype(F32)
            low_ref[here, h * 128 : (h + 1) * 128] = (picks & 255).astype(F32)
        return carry

    lax.fori_loop(0, idx_ref.shape[1] // 256, eight_groups, 0)


def count_group(key_ref, low_ref, iota_ref, group):
    iota = iota_ref[...]
    one, zero = jnp.ones((), BF), jnp.zeros((), BF)
    hot = []
    for ref in (key_ref, low_ref):
        row = jnp.broadcast_to(ref[pl.ds(group, 1), :], (16, LOW)).astype(BF)
        hot.append(jnp.where(jnp.concatenate([row] * 16, 0) == iota, one, zero))
    return dot(hot[0], hot[1], ((1,), (1,))).astype(BF)


def put_counts(count_ref, where, row, counts):
    for h in range(8):
        count_ref[where, pl.ds(row, BAG_GROUP), h * LOW : (h + 1) * LOW] = counts[h * 32 : (h + 1) * 32]


def step_kernel(names, n_node, n_local, *refs):
    r = types.SimpleNamespace(**dict(zip(names, refs)))
    node, lane = lax.axis_index("node"), lax.axis_index("local")
    chips = n_local // 2
    chip, core = lane // 2, lax.rem(lane, 2)
    sibling = chip * 2 + 1 - core
    cap, small = r.packed.shape[2], r.packed.shape[3]
    samples, total = r.x.shape
    half = samples // HALVES
    share = half // n_local
    width = r.gpre.shape[3]
    per_node = samples // BAG_GROUP
    groups = small // BAG_GROUP
    at_once = CHUNK // groups
    chunks = n_node // at_once
    arrived = [getattr(r, f"arrived{p}") for p in range(PIECES)]
    landed = [getattr(r, f"landed{p}") for p in range(PIECES)]
    returned = [getattr(r, f"returned{p}") for p in range(PIECES)]

    def rows(h):
        return slice(h * half, (h + 1) * half)

    def each(count, act, first=0):
        def body(i, carry):
            act(i)
            return carry

        lax.fori_loop(first, count, body, 0)

    def remote(src, dst, sems, at, peer):
        send, recv = sems
        return pltpu.make_async_remote_copy(
            src_ref=src, dst_ref=dst, send_sem=send.at[at], recv_sem=recv.at[at], device_id=peer, device_id_type=MESH
        )

    def node_peer(k):
        return lax.rem(node + k, n_node), lane

    def lane_peer(d):
        return node, lax.rem(lane + d, n_local)

    def chip_peer(dy):
        return node, lax.rem(chip + dy, chips) * 2 + core

    def find_slots():
        features = r.owner.shape[1]
        wide = (features, features)
        here = jnp.broadcast_to(r.owner[...].astype(F32), wide)
        owner, other = here.T.astype(jnp.int32), here.astype(jnp.int32)
        feature, at = lax.broadcasted_iota(jnp.int32, wide, 0), lax.broadcasted_iota(jnp.int32, wide, 1)
        group, other_group = feature // n_node, at // n_node
        own_lane, own_node = lax.rem(owner, n_local), owner // n_local
        ahead = (at < feature) & (group == other_group) & (lax.rem(other, n_local) == own_lane)
        rank = jnp.sum(ahead.astype(F32), axis=1, keepdims=True).astype(jnp.int32)
        source_slot, target_slot = group * cap + rank, own_lane * cap + rank

        def put(row, where, value, limit):
            chosen = jnp.where(where, value, 0).astype(F32)
            found = jnp.sum(chosen, axis=0, keepdims=True).astype(jnp.int32)
            r.slots_v[row : row + 1, :] = jnp.clip(found, 0, limit - 1)

        put(0, (own_lane == lane) & (source_slot == at), own_node, n_node)
        put(1, feature == lane * n_node + at, target_slot, n_local * cap)
        put(2, (group == lane) & (target_slot == at), feature - lane * n_node, n_node)
        put(3, owner == at * n_local + lane, source_slot, n_local * cap)
        copy = pltpu.make_async_copy(r.slots_v, r.slots, r.load_sem.at[7])
        copy.start()
        copy.wait()

    def out_node(p, k):
        return remote(r.pooled.at[p, k], arrived[p].at[node], (r.on_s, r.on_r), (p, k), node_peer(k))

    def out_lane(p, d):
        here = pl.ds(lane * cap, cap)
        return remote(r.packed.at[p, d], landed[p].at[here], (r.ol_s, r.ol_r), (p, d), lane_peer(d))

    def back_lane(p, d):
        here = pl.ds(lane * cap, cap)
        return remote(r.packed.at[p, d], returned[p].at[here], (r.bl_s, r.bl_r), (p, d), lane_peer(d))

    def back_node(p, k):
        return remote(r.pooled.at[p, k], r.home.at[p, node], (r.bn_s, r.bn_r), (p, k), node_peer(k))

    def part_to(w, h, d):
        peer = lane_peer(d)
        return remote(r.rank_send.at[w, h, peer[1]], r.rank_recv.at[w, h, lane], (r.rk_s, r.rk_r), (w, h, d), peer)

    def share_to(w, h, d):
        return remote(r.rank.at[w, h, lane], r.rank.at[w, h, lane], (r.sh_s, r.sh_r), (w, h, d), lane_peer(d))

    def to_sibling(h, y):
        return remote(r.sib_send.at[h, y], r.sib_recv.at[h, y], (r.sb_s, r.sb_r), (h, y), (node, sibling))

    def pre_to(h, dy):
        return remote(r.pre_send.at[h, dy], r.pre_recv.at[h, dy], (r.pr_s, r.pr_r), (h, dy), chip_peer(dy))

    def gpre_to(h, dy):
        return remote(r.gpre.at[h, lane], r.gpre.at[h, lane], (r.gp_s, r.gp_r), (h, dy), chip_peer(dy))

    def forward(h, dy):
        source = lax.rem(chip + chips - dy, chips) * 2 + core
        return remote(r.gpre.at[h, source], r.gpre.at[h, source], (r.fw_s, r.fw_r), (h, dy), (node, sibling))

    def save(t):
        buffer = lax.rem(t, 2)
        return pltpu.make_async_copy(r.counts.at[buffer], r.kept.at[t], r.save_sem.at[buffer])

    def fetch(t):
        buffer = lax.rem(t, 2)
        return pltpu.make_async_copy(r.kept.at[t], r.counts.at[buffer], r.fetch_sem.at[buffer])

    def pool_chunk(p, c):
        t = p * chunks + c

        @pl.when(t >= 2)
        def _():
            save(t - 2).wait()

        buffer = lax.rem(t, 2)
        for i in range(CHUNK):
            source = lax.rem(node + c * at_once + i // groups, n_node)
            group = source * per_node + p * groups + i % groups
            put_counts(r.counts, buffer, i * BAG_GROUP, count_group(r.key, r.low, r.iota, group))
        save(t).start()
        sums = dot(r.counts[buffer], r.table[...]).astype(BF)
        for i in range(at_once):
            r.pooled[p, c * at_once + i] = sums[i * small : (i + 1) * small]

    def send_chunk(p, c):
        each((c + 1) * at_once, lambda k: out_node(p, k).start(), jnp.maximum(c * at_once, 1))

    def pack_piece(p):
        each(n_node, lambda k: out_node(p, k).wait_recv(), 1)
        arrived[p][node] = r.pooled[p, 0]

        def send(d):
            target = lax.rem(lane + d, n_local)
            for c in range(cap):
                r.packed[p, d, c] = arrived[p][r.slots[0, target * cap + c]]
            out_lane(p, d).start()

        each(n_local, send, 1)
        for c in range(cap):
            landed[p][lane * cap + c] = arrived[p][r.slots[0, lane * cap + c]]

    def unpack_piece(p):
        each(n_local, lambda d: out_lane(p, d).wait_recv(), 1)
        for q in range(n_node):
            r.x[p * small : (p + 1) * small, q * 128 : (q + 1) * 128] = landed[p][r.slots[1, q]]

    def lay_up():
        depth = r.up.shape[0] // r.gx.shape[0]

        def block(i):
            turned = jnp.swapaxes(r.gx[i].reshape(depth, n_node, 128), 0, 1)
            for q in range(n_node):
                r.up[pl.ds(pl.multiple_of(i * depth, depth), depth), q * 128 : (q + 1) * 128] = turned[q]

        each(r.gx.shape[0], block)

    def send_parts(w, h, part):
        def columns(n):
            here = pl.ds(pl.multiple_of(n * 256, 256), 256)
            piece = part(here).astype(BF)
            for t in range(n_local):
                r.rank_send[w, h, t, :, here] = piece[t * share : (t + 1) * share]

        each(r.rank.shape[4] // 256, columns)
        each(n_local, lambda d: part_to(w, h, d).start(), 1)

    def reduce_parts(w, h):
        r.rank_recv[w, h, lane] = r.rank_send[w, h, lane]
        each(n_local, lambda d: part_to(w, h, d).wait_recv(), 1)
        summed = r.rank_recv[w, h, 0].astype(F32)
        for t in range(1, n_local):
            summed = summed + r.rank_recv[w, h, t].astype(F32)
        r.rank[w, h, lane] = summed.astype(BF)
        each(n_local, lambda d: share_to(w, h, d).start(), 1)

    def whole_rank(w, h):
        return r.rank[w, h].reshape(half, r.rank.shape[4])

    def side_by_side(ref, h):
        return jnp.concatenate([ref[q, rows(h), :] for q in range(n_node)], 1)

    def low_parts(h):
        send_parts(0, h, lambda here: dot(r.x[rows(h), :], r.down[:, here]))

    def cross(h):
        each(n_local, lambda d: share_to(0, h, d).wait_recv(), 1)

        def columns(n):
            here = pl.ds(pl.multiple_of(n * 512, 512), 512)
            added = dot(whole_rank(0, h), r.up[:, here]) + r.bias[:, here]
            x = r.x[rows(h), here].astype(F32)
            result = (x * added + x).astype(BF)
            r.term[rows(h), here] = added
            for i in range(4):
                r.crossed[n * 4 + i, rows(h), :] = result[:, i * 128 : (i + 1) * 128]

        each(total // 512, columns)
        keep_crossed(h).start()

    def keep_crossed(h):
        return pltpu.make_async_copy(r.crossed.at[:, rows(h)], r.crossed_out.at[:, rows(h)], r.out_sem.at[h])

    def pre(h):
        def part(t):
            return dot(side_by_side(r.crossed, h), r.weight[:, pl.ds(pl.multiple_of(t * width, width), width)])

        def other_core(y):
            r.sib_send[h, y] = part(y * 2 + 1 - core).astype(BF)
            to_sibling(h, y).start()

        def my_core(i):
            dy = lax.rem(i + 1, chips)
            y = lax.rem(chip + dy, chips)
            mine = part(y * 2 + core)
            to_sibling(h, y).wait_recv()
            mine = mine + r.sib_recv[h, y].astype(F32)

            @pl.when(dy == 0)
            def _():
                r.pre_own[h] = mine

            @pl.when(dy > 0)
            def _():
                r.pre_send[h, dy] = mine.astype(BF)
                pre_to(h, dy).start()

        each(chips, other_core)
        each(chips, my_core)

    def activate(h):
        value = r.pre_own[h] + r.hbias[:, pl.ds(pl.multiple_of(lane * width, width), width)]
        for dy in range(1, chips):
            pre_to(h, dy).wait_recv()
            value = value + r.pre_recv[h, dy].astype(F32)
        sig = jax.nn.sigmoid(value)
        r.hidden[rows(h), :] = (value * sig).astype(BF)
        r.gpre[h, lane] = (r.hgrad[rows(h), :].astype(F32) * sig * (1.0 + value * (1.0 - sig))).astype(BF)
        each(chips, lambda dy: gpre_to(h, dy).start(), 1)
        forward(h, 0).start()

    def pass_on(h):
        def one(dy):
            gpre_to(h, dy).wait_recv()
            forward(h, dy).start()

        each(chips, one, 1)

    def back_chips(h, steps):
        sides = []
        for dy in steps:
            forward(h, dy).wait_recv()
            y = lax.rem(chip + chips - dy, chips)
            wide = pl.ds(pl.multiple_of(y * 2 * width, 2 * width), 2 * width)
            sides.append((y, wide))

        def columns(n):
            here = pl.ds(pl.multiple_of(n * 512, 512), 512)
            added = None
            for y, wide in sides:
                grads = jnp.concatenate([r.gpre[h, y * 2], r.gpre[h, y * 2 + 1]], 1)
                term = dot(grads, r.weight[here, wide], ((1,), (1,)))
                added = term if added is None else added + term
            if 0 in steps:
                r.gcross[rows(h), here] = added
            else:
                r.gcross[rows(h), here] += added

        each(total // 512, columns)

    def rank_grad(h):
        for q in range(n_node):
            here = slice(q * 128, (q + 1) * 128)
            r.gx[q, rows(h), :] = (r.gcross[rows(h), here] * r.x[rows(h), here].astype(F32)).astype(BF)
        send_parts(1, h, lambda here: dot(side_by_side(r.gx, h), r.up[here, :], ((1,), (1,))))

    def input_grad(h):
        each(n_local, lambda d: share_to(1, h, d).wait_recv(), 1)

        def columns(n):
            here = pl.ds(pl.multiple_of(n * 512, 512), 512)
            grads = r.gcross[rows(h), here]
            result = grads * r.term[rows(h), here] + grads + dot(whole_rank(1, h), r.down[here, :], ((1,), (1,)))
            result = result.astype(BF)
            for i in range(4):
                r.gx[n * 4 + i, rows(h), :] = result[:, i * 128 : (i + 1) * 128]

        each(total // 512, columns)

    def pack_back(p):
        here = slice(p * small, (p + 1) * small)
        each(n_local, lambda d: out_lane(p, d).wait_send(), 1)

        def send(d):
            target = lax.rem(lane + d, n_local)
            for c in range(cap):
                r.packed[p, d, c] = r.gx[r.slots[2, target * cap + c], here]
            back_lane(p, d).start()

        each(n_local, send, 1)
        for c in range(cap):
            returned[p][lane * cap + c] = r.gx[r.slots[2, lane * cap + c], here]

    def route_piece(p):
        each(n_node, lambda k: out_node(p, k).wait_send(), 1)
        each(n_local, lambda d: back_lane(p, d).wait_recv(), 1)

        def send(k):
            r.pooled[p, k] = returned[p][r.slots[3, lax.rem(node + k, n_node)]]
            back_node(p, k).start()

        each(n_node, send, 1)
        r.home[p, node] = returned[p][r.slots[3, node]]

    def add_piece(p):
        each(n_node, lambda k: back_node(p, k).wait_recv(), 1)

        def one_chunk(c):
            t = p * chunks + c
            buffer = lax.rem(t, 2)
            for i in range(at_once * small // 128):
                parts = [
                    r.home[p, lax.rem(node + c * at_once + i * (128 // small) + j, n_node)] for j in range(128 // small)
                ]
                r.home_t[:, i * 128 : (i + 1) * 128] = jnp.concatenate(parts, 0).T
            fetch(t).wait()
            for n in range(r.sums.shape[1] // 512):
                here = slice(n * 512, (n + 1) * 512)
                r.sums[:, here] += dot(r.home_t[...], r.counts[buffer, :, here])

            @pl.when(t + 2 < PIECES * chunks)
            def _():
                fetch(t + 2).start()

        each(chunks, one_chunk)

    my_columns = pl.ds(pl.multiple_of(lane * width, width), width)
    loads = [
        pltpu.make_async_copy(r.down_hbm, r.down, r.load_sem.at[0]),
        pltpu.make_async_copy(r.up_hbm, r.gx, r.load_sem.at[1]),
        pltpu.make_async_copy(r.weight_hbm, r.weight, r.load_sem.at[2]),
        pltpu.make_async_copy(r.grad_hbm.at[:, my_columns], r.hgrad, r.load_sem.at[3]),
    ]
    barrier = greet(n_node, n_local, node, lane)
    fill = [
        pltpu.make_async_copy(r.idx_hbm, r.idx, r.load_sem.at[4]),
        pltpu.make_async_copy(r.size_hbm, r.size, r.load_sem.at[5]),
        pltpu.make_async_copy(r.table_hbm, r.table, r.load_sem.at[6]),
    ]
    for load in fill:
        load.start()
    r.slots_v[...] = jnp.zeros_like(r.slots_v)
    find_slots()
    for load in fill:
        load.wait()
    for load in loads:
        load.start()
    flatten_picks(r.idx, r.size, r.iota, r.key, r.low)
    each(chunks, lambda c: pool_chunk(0, c))
    pl.semaphore_wait(barrier, n_node + n_local - 2)
    for c in range(chunks):
        send_chunk(0, c)

    def turn(p):
        def one_chunk(c):
            pool_chunk(p, c)
            for piece in range(1, PIECES):

                @pl.when(p == piece)
                def _():
                    send_chunk(piece, c)

        each(chunks, one_chunk)
        for piece in range(PIECES - LAG):

            @pl.when(p == piece + LAG)
            def _():
                pack_piece(piece)

    each(PIECES, turn, 1)
    r.sums[...] = jnp.zeros_like(r.sums)
    for t in range(2):
        save(PIECES * chunks - 2 + t).wait()
    for t in range(2):
        fetch(t).start()
    for load in loads:
        load.wait()
    unpack_piece(0)
    unpack_piece(1)
    unpack_piece(3)
    unpack_piece(2)
    low_parts(0)
    pack_piece(6)
    unpack_piece(5)
    unpack_piece(4)
    lay_up()
    reduce_parts(0, 0)
    pack_piece(7)
    unpack_piece(6)
    cross(0)
    pre(0)
    unpack_piece(7)
    low_parts(1)
    activate(0)
    back_chips(0, [0])
    pass_on(0)
    reduce_parts(0, 1)
    back_chips(0, [1, 2, 3])
    rank_grad(0)
    cross(1)
    pre(1)
    reduce_parts(1, 0)
    activate(1)
    back_chips(1, [0])
    input_grad(0)
    pack_back(0)
    pack_back(1)
    pass_on(1)
    back_chips(1, [1, 2, 3])
    rank_grad(1)
    route_piece(0)
    pack_back(2)
    reduce_parts(1, 1)
    pack_back(3)
    route_piece(2)
    route_piece(1)
    input_grad(1)
    pack_back(4)
    route_piece(3)
    pack_back(5)
    route_piece(4)
    pack_back(6)
    add_piece(0)
    add_piece(1)
    pack_back(7)
    route_piece(5)
    route_piece(6)
    add_piece(2)
    route_piece(7)
    add_piece(3)
    add_piece(4)
    add_piece(5)
    add_piece(6)
    add_piece(7)
    for n in range(r.sums.shape[1] // 128):
        r.table_grad[n * 128 : (n + 1) * 128, :] = r.sums[:, n * 128 : (n + 1) * 128].T

    for p in range(PIECES):
        each(n_node, lambda k: back_node(p, k).wait_send(), 1)
        each(n_local, lambda d: back_lane(p, d).wait_send(), 1)
    for h in range(HALVES):
        keep_crossed(h).wait()
        for w in range(2):
            each(n_local, lambda d: part_to(w, h, d).wait_send(), 1)
            each(n_local, lambda d: share_to(w, h, d).wait_send(), 1)
        each(chips, lambda y: to_sibling(h, y).wait_send())
        each(chips, lambda dy: pre_to(h, dy).wait_send(), 1)
        each(chips, lambda dy: gpre_to(h, dy).wait_send(), 1)
        each(chips, lambda dy: forward(h, dy).wait_send())


VMEM = pl.BlockSpec(memory_space=pltpu.VMEM)
ANY = pl.BlockSpec(memory_space=pl.ANY)
SEM = pltpu.SemaphoreType.DMA


def train_step(operands, features, samples, n_node, n_local, cap):
    depth, hidden = operands["down_hbm"].shape[1], operands["weight_hbm"].shape[1]
    total = operands["down_hbm"].shape[0]
    table_rows, emb = operands["table_hbm"].shape
    groups = operands["idx_hbm"].shape[1] // BAG_GROUP
    small, half, width, chips = samples // PIECES, samples // HALVES, hidden // n_local, n_local // 2
    kept = (groups // CHUNK, CHUNK * BAG_GROUP, table_rows)
    outs = {
        "crossed_out": (jax.ShapeDtypeStruct((features, samples, emb), BF), ANY),
        "hidden": (jax.ShapeDtypeStruct((samples, width), BF), VMEM),
        "table_grad": (jax.ShapeDtypeStruct((table_rows, emb), F32), VMEM),
        "kept": (jax.ShapeDtypeStruct(kept, BF), ANY),
    }
    parts = pltpu.VMEM((2, HALVES, n_local, half // n_local, depth), BF)
    quarter = pltpu.VMEM((HALVES, chips, half, width), BF)
    scratch = {
        "idx": pltpu.VMEM(operands["idx_hbm"].shape, jnp.int32),
        "size": pltpu.VMEM(operands["size_hbm"].shape, jnp.int32),
        "table": pltpu.VMEM((table_rows, emb), BF),
        "slots_v": pltpu.VMEM((8, operands["owner"].shape[1]), jnp.int32),
        "slots": pltpu.SMEM((8, operands["owner"].shape[1]), jnp.int32),
        "iota": pltpu.VMEM((LOW, LOW), BF),
        "key": pltpu.VMEM((groups, LOW), F32),
        "low": pltpu.VMEM((groups, LOW), F32),
        "counts": pltpu.VMEM((2, *kept[1:]), BF),
        "pooled": pltpu.VMEM((PIECES, n_node, small, emb), BF),
        "packed": pltpu.VMEM((PIECES, n_local, cap, small, emb), BF),
        "home": pltpu.VMEM((PIECES, n_node, small, emb), BF),
        "home_t": pltpu.VMEM((emb, kept[1]), BF),
        "sums": pltpu.VMEM((emb, table_rows), F32),
        "x": pltpu.VMEM((samples, total), BF),
        "down": pltpu.VMEM((total, depth), BF),
        "up": pltpu.VMEM((depth, total), BF),
        "weight": pltpu.VMEM((total, hidden), BF),
        "hgrad": pltpu.VMEM((samples, width), BF),
        "term": pltpu.VMEM((samples, total), F32),
        "gcross": pltpu.VMEM((samples, total), F32),
        "gx": pltpu.VMEM((features, samples, emb), BF),
        "crossed": pltpu.VMEM((features, samples, emb), BF),
        "out_sem": SEM((HALVES,)),
        "rank_send": parts,
        "rank_recv": parts,
        "rank": parts,
        "sib_send": quarter,
        "sib_recv": quarter,
        "pre_send": quarter,
        "pre_recv": quarter,
        "pre_own": pltpu.VMEM((HALVES, half, width), F32),
        "gpre": pltpu.VMEM((HALVES, n_local, half, width), BF),
        "load_sem": SEM((8,)),
        "save_sem": SEM((2,)),
        "fetch_sem": SEM((2,)),
    }
    for p in range(PIECES):
        scratch[f"arrived{p}"] = pltpu.VMEM((n_node, small, emb), BF)
        scratch[f"landed{p}"] = pltpu.VMEM((n_local * cap, small, emb), BF)
        scratch[f"returned{p}"] = pltpu.VMEM((n_local * cap, small, emb), BF)
    for names, shape in (
        (("on", "bn"), (PIECES, n_node)),
        (("ol", "bl"), (PIECES, n_local)),
        (("rk", "sh"), (2, HALVES, n_local)),
        (("sb", "pr", "gp", "fw"), (HALVES, chips)),
    ):
        for name in names:
            scratch[name + "_s"] = SEM(shape)
            scratch[name + "_r"] = SEM(shape)
    specs = [ANY if name.endswith("_hbm") else VMEM for name in operands]
    names = [*operands, *outs, *scratch]
    return pl.pallas_call(
        functools.partial(step_kernel, names, n_node, n_local),
        out_shape=[shape for shape, _ in outs.values()],
        in_specs=specs,
        out_specs=[spec for _, spec in outs.values()],
        scratch_shapes=list(scratch.values()),
        compiler_params=pltpu.CompilerParams(collective_id=0, has_side_effects=True, vmem_limit_bytes=VMEM_LIMIT),
        name="train_step",
    )(*operands.values())


def hand_out_kernel(count, *refs):
    given, taken, held = refs[:count], refs[count : 2 * count], refs[2 * count : 3 * count]
    read_sem, write_sem = refs[3 * count :]
    reads, writes = [], []
    for source, target, middle in zip(given, taken, held):
        rows = source.shape[0] // 4
        for i in range(4):
            part, at = pl.ds(i * rows, rows), len(reads)
            reads.append(pltpu.make_async_copy(source.at[part], middle.at[part], read_sem.at[at]))
            writes.append(pltpu.make_async_copy(middle.at[part], target.at[part], write_sem.at[at]))
    for copy in reads:
        copy.start()
    for read, write in zip(reads, writes):
        read.wait()
        write.start()
    for copy in writes:
        copy.wait()


def hand_out(*arrays):
    count = len(arrays)
    return pl.pallas_call(
        functools.partial(hand_out_kernel, count),
        out_shape=[jax.ShapeDtypeStruct(a.shape, a.dtype) for a in arrays],
        in_specs=[ANY] * count,
        out_specs=[ANY] * count,
        scratch_shapes=[*[pltpu.VMEM(a.shape, a.dtype) for a in arrays], SEM((4 * count,)), SEM((4 * count,))],
        compiler_params=pltpu.CompilerParams(vmem_limit_bytes=VMEM_LIMIT),
        name="hand_out",
    )(*arrays)


def on_device(
    owner_map,
    bag_sizes,
    indices,
    tables,
    cross_down,
    cross_up,
    cross_bias,
    mlp_weight,
    mlp_bias,
    hidden_grad,
):
    node_count = lax.axis_size("node")
    lane_count = lax.axis_size("local")
    capacity = node_count // lane_count + 1
    samples = hidden_grad.shape[0]
    hidden_width = hidden_grad.shape[1]
    operands = {
        "owner": owner_map.reshape(1, -1),
        "bias": cross_bias.reshape(1, -1),
        "hbias": mlp_bias.reshape(1, -1),
        "idx_hbm": indices[0].T,
        "size_hbm": bag_sizes,
        "table_hbm": tables,
        "grad_hbm": hidden_grad,
        "down_hbm": cross_down.reshape(-1, cross_down.shape[2]),
        "up_hbm": cross_up.reshape(node_count, -1, cross_up.shape[2]),
        "weight_hbm": mlp_weight.reshape(-1, hidden_width),
    }
    crossed, hidden, table_grad, _ = train_step(operands, node_count, samples, node_count, lane_count, capacity)
    return hand_out(crossed, hidden, table_grad)


def solution(mesh):
    return jax.shard_map(
        on_device,
        mesh=mesh,
        in_specs=(
            P(),
            P(("node", "local"), None),
            P(("node", "local"), None, None),
            P(("node", "local"), None),
            P("local", None, None),
            P(None, "local", None),
            P("local", None),
            P("local", None, None),
            P(),
            P("node", None),
        ),
        out_specs=(P("local", "node", None), P("node", "local"), P(("node", "local"), None)),
        check_vma=False,
    )
```

```python
import functools
import types

import jax
import jax.numpy as jnp
from jax import lax
from jax.experimental import pallas as pl
from jax.experimental.pallas import tpu as pltpu
from jax.sharding import PartitionSpec as P

BF = jnp.bfloat16
F32 = jnp.float32
MESH = pl.DeviceIdType.MESH
PIECES = 8
HALVES = 2
CHUNK = 16
LAG = 2
VMEM_LIMIT = 62 << 20
BAG_GROUP = 32
LOW = 256


def dot(a, b, contract=((1,), (0,))):
    return lax.dot_general(a, b, (contract, ((), ())), preferred_element_type=F32)


def greet(n_node, n_local, node, lane):
    barrier = pltpu.get_barrier_semaphore()

    def by_node(k, carry):
        peer = lax.rem(node + k, n_node)
        pl.semaphore_signal(barrier, inc=1, device_id=(peer, lane), device_id_type=MESH)
        return carry

    def by_lane(d, carry):
        peer = lax.rem(lane + d, n_local)
        pl.semaphore_signal(barrier, inc=1, device_id=(node, peer), device_id_type=MESH)
        return carry

    lax.fori_loop(1, n_node, by_node, 0)
    lax.fori_loop(1, n_local, by_lane, 0)
    return barrier


def flatten_picks(idx_ref, size_ref, iota_ref, key_ref, low_ref):
    iota_ref[...] = lax.broadcasted_iota(jnp.int32, iota_ref.shape, 0).astype(F32).astype(BF)
    lanes = lax.broadcasted_iota(jnp.int32, (1, 128), 1)
    depth = lax.broadcasted_iota(jnp.int32, (8, 128), 0)

    def eight_groups(b, carry):
        rows = [[], []]
        for half in range(2):
            off = pl.multiple_of(b * 256 + half * 128, 128)
            picks = jnp.where(depth < size_ref[:, pl.ds(off, 128)], idx_ref[:, pl.ds(off, 128)], -1)
            turned = [picks] + [pltpu.roll(picks, 32 * d, 1) for d in (1, 2, 3)]
            for group in range(4):
                for h in range(2):
                    row = turned[(3 - group) % 4][4 * h + 3 : 4 * h + 4]
                    for q in (2, 1, 0):
                        source = turned[(q - group) % 4][4 * h + q : 4 * h + q + 1]
                        row = jnp.where(lanes < 32 * (q + 1), source, row)
                    rows[h].append(row)
        here = pl.ds(pl.multiple_of(b * 8, 8), 8)
        for h in range(2):
            picks = jnp.concatenate(rows[h], 0)
            key_ref[here, h * 128 : (h + 1) * 128] = ((picks >> 8) * 32 + (lanes & 31)).astype(F32)
            low_ref[here, h * 128 : (h + 1) * 128] = (picks & 255).astype(F32)
        return carry

    lax.fori_loop(0, idx_ref.shape[1] // 256, eight_groups, 0)


def count_group(key_ref, low_ref, iota_ref, group):
    iota = iota_ref[...]
    one, zero = jnp.ones((), BF), jnp.zeros((), BF)
    hot = []
    for ref in (key_ref, low_ref):
        row = jnp.broadcast_to(ref[pl.ds(group, 1), :], (16, LOW)).astype(BF)
        hot.append(jnp.where(jnp.concatenate([row] * 16, 0) == iota, one, zero))
    return dot(hot[0], hot[1], ((1,), (1,))).astype(BF)


def put_counts(count_ref, where, row, counts):
    for h in range(8):
        count_ref[where, pl.ds(row, BAG_GROUP), h * LOW : (h + 1) * LOW] = counts[h * 32 : (h + 1) * 32]


def step_kernel(names, n_node, n_local, *refs):
    r = types.SimpleNamespace(**dict(zip(names, refs)))
    node, lane = lax.axis_index("node"), lax.axis_index("local")
    chips = n_local // 2
    chip, core = lane // 2, lax.rem(lane, 2)
    sibling = chip * 2 + 1 - core
    cap, small = r.packed.shape[2], r.packed.shape[3]
    samples, total = r.x.shape
    half = samples // HALVES
    share = half // n_local
    width = r.gpre.shape[3]
    per_node = samples // BAG_GROUP
    groups = small // BAG_GROUP
    at_once = CHUNK // groups
    chunks = n_node // at_once
    arrived = [getattr(r, f"arrived{p}") for p in range(PIECES)]
    landed = [getattr(r, f"landed{p}") for p in range(PIECES)]
    returned = [getattr(r, f"returned{p}") for p in range(PIECES)]

    def rows(h):
        return slice(h * half, (h + 1) * half)

    def each(count, act, first=0):
        def body(i, carry):
            act(i)
            return carry

        lax.fori_loop(first, count, body, 0)

    def remote(src, dst, sems, at, peer):
        send, recv = sems
        return pltpu.make_async_remote_copy(
            src_ref=src, dst_ref=dst, send_sem=send.at[at], recv_sem=recv.at[at], device_id=peer, device_id_type=MESH
        )

    def node_peer(k):
        return lax.rem(node + k, n_node), lane

    def lane_peer(d):
        return node, lax.rem(lane + d, n_local)

    def chip_peer(dy):
        return node, lax.rem(chip + dy, chips) * 2 + core

    def find_slots():
        features = r.owner.shape[1]
        wide = (features, features)
        here = jnp.broadcast_to(r.owner[...].astype(F32), wide)
        owner, other = here.T.astype(jnp.int32), here.astype(jnp.int32)
        feature, at = lax.broadcasted_iota(jnp.int32, wide, 0), lax.broadcasted_iota(jnp.int32, wide, 1)
        group, other_group = feature // n_node, at // n_node
        own_lane, own_node = lax.rem(owner, n_local), owner // n_local
        ahead = (at < feature) & (group == other_group) & (lax.rem(other, n_local) == own_lane)
        rank = jnp.sum(ahead.astype(F32), axis=1, keepdims=True).astype(jnp.int32)
        source_slot, target_slot = group * cap + rank, own_lane * cap + rank

        def put(row, where, value, limit):
            chosen = jnp.where(where, value, 0).astype(F32)
            found = jnp.sum(chosen, axis=0, keepdims=True).astype(jnp.int32)
            r.slots_v[row : row + 1, :] = jnp.clip(found, 0, limit - 1)

        put(0, (own_lane == lane) & (source_slot == at), own_node, n_node)
        put(1, feature == lane * n_node + at, target_slot, n_local * cap)
        put(2, (group == lane) & (target_slot == at), feature - lane * n_node, n_node)
        put(3, owner == at * n_local + lane, source_slot, n_local * cap)
        copy = pltpu.make_async_copy(r.slots_v, r.slots, r.load_sem.at[7])
        copy.start()
        copy.wait()

    def out_node(p, k):
        return remote(r.pooled.at[p, k], arrived[p].at[node], (r.on_s, r.on_r), (p, k), node_peer(k))

    def out_lane(p, d):
        here = pl.ds(lane * cap, cap)
        return remote(r.packed.at[p, d], landed[p].at[here], (r.ol_s, r.ol_r), (p, d), lane_peer(d))

    def back_lane(p, d):
        here = pl.ds(lane * cap, cap)
        return remote(r.packed.at[p, d], returned[p].at[here], (r.bl_s, r.bl_r), (p, d), lane_peer(d))

    def back_node(p, k):
        return remote(r.pooled.at[p, k], r.home.at[p, node], (r.bn_s, r.bn_r), (p, k), node_peer(k))

    def part_to(w, h, d):
        peer = lane_peer(d)
        return remote(r.rank_send.at[w, h, peer[1]], r.rank_recv.at[w, h, lane], (r.rk_s, r.rk_r), (w, h, d), peer)

    def share_to(w, h, d):
        return remote(r.rank.at[w, h, lane], r.rank.at[w, h, lane], (r.sh_s, r.sh_r), (w, h, d), lane_peer(d))

    def to_sibling(h, y):
        return remote(r.sib_send.at[h, y], r.sib_recv.at[h, y], (r.sb_s, r.sb_r), (h, y), (node, sibling))

    def pre_to(h, dy):
        return remote(r.pre_send.at[h, dy], r.pre_recv.at[h, dy], (r.pr_s, r.pr_r), (h, dy), chip_peer(dy))

    def gpre_to(h, dy):
        return remote(r.gpre.at[h, lane], r.gpre.at[h, lane], (r.gp_s, r.gp_r), (h, dy), chip_peer(dy))

    def forward(h, dy):
        source = lax.rem(chip + chips - dy, chips) * 2 + core
        return remote(r.gpre.at[h, source], r.gpre.at[h, source], (r.fw_s, r.fw_r), (h, dy), (node, sibling))

    def save(t):
        buffer = lax.rem(t, 2)
        return pltpu.make_async_copy(r.counts.at[buffer], r.kept.at[t], r.save_sem.at[buffer])

    def fetch(t):
        buffer = lax.rem(t, 2)
        return pltpu.make_async_copy(r.kept.at[t], r.counts.at[buffer], r.fetch_sem.at[buffer])

    def pool_chunk(p, c):
        t = p * chunks + c

        @pl.when(t >= 2)
        def _():
            save(t - 2).wait()

        buffer = lax.rem(t, 2)
        for i in range(CHUNK):
            source = lax.rem(node + c * at_once + i // groups, n_node)
            group = source * per_node + p * groups + i % groups
            put_counts(r.counts, buffer, i * BAG_GROUP, count_group(r.key, r.low, r.iota, group))
        save(t).start()
        sums = dot(r.counts[buffer], r.table[...]).astype(BF)
        for i in range(at_once):
            r.pooled[p, c * at_once + i] = sums[i * small : (i + 1) * small]

    def send_chunk(p, c):
        each((c + 1) * at_once, lambda k: out_node(p, k).start(), jnp.maximum(c * at_once, 1))

    def pack_piece(p):
        each(n_node, lambda k: out_node(p, k).wait_recv(), 1)
        arrived[p][node] = r.pooled[p, 0]

        def send(d):
            target = lax.rem(lane + d, n_local)
            for c in range(cap):
                r.packed[p, d, c] = arrived[p][r.slots[0, target * cap + c]]
            out_lane(p, d).start()

        each(n_local, send, 1)
        for c in range(cap):
            landed[p][lane * cap + c] = arrived[p][r.slots[0, lane * cap + c]]

    def unpack_piece(p):
        each(n_local, lambda d: out_lane(p, d).wait_recv(), 1)
        for q in range(n_node):
            r.x[p * small : (p + 1) * small, q * 128 : (q + 1) * 128] = landed[p][r.slots[1, q]]

    def lay_up():
        depth = r.up.shape[0] // r.gx.shape[0]

        def block(i):
            turned = jnp.swapaxes(r.gx[i].reshape(depth, n_node, 128), 0, 1)
            for q in range(n_node):
                r.up[pl.ds(pl.multiple_of(i * depth, depth), depth), q * 128 : (q + 1) * 128] = turned[q]

        each(r.gx.shape[0], block)

    def send_parts(w, h, part):
        def columns(n):
            here = pl.ds(pl.multiple_of(n * 256, 256), 256)
            piece = part(here).astype(BF)
            for t in range(n_local):
                r.rank_send[w, h, t, :, here] = piece[t * share : (t + 1) * share]

        each(r.rank.shape[4] // 256, columns)
        each(n_local, lambda d: part_to(w, h, d).start(), 1)

    def reduce_parts(w, h):
        r.rank_recv[w, h, lane] = r.rank_send[w, h, lane]
        each(n_local, lambda d: part_to(w, h, d).wait_recv(), 1)
        summed = r.rank_recv[w, h, 0].astype(F32)
        for t in range(1, n_local):
            summed = summed + r.rank_recv[w, h, t].astype(F32)
        r.rank[w, h, lane] = summed.astype(BF)
        each(n_local, lambda d: share_to(w, h, d).start(), 1)

    def whole_rank(w, h):
        return r.rank[w, h].reshape(half, r.rank.shape[4])

    def side_by_side(ref, h):
        return jnp.concatenate([ref[q, rows(h), :] for q in range(n_node)], 1)

    def low_parts(h):
        send_parts(0, h, lambda here: dot(r.x[rows(h), :], r.down[:, here]))

    def cross(h):
        each(n_local, lambda d: share_to(0, h, d).wait_recv(), 1)

        def columns(n):
            here = pl.ds(pl.multiple_of(n * 512, 512), 512)
            added = dot(whole_rank(0, h), r.up[:, here]) + r.bias[:, here]
            x = r.x[rows(h), here].astype(F32)
            result = (x * added + x).astype(BF)
            r.term[rows(h), here] = added
            for i in range(4):
                r.crossed[n * 4 + i, rows(h), :] = result[:, i * 128 : (i + 1) * 128]

        each(total // 512, columns)
        keep_crossed(h).start()

    def keep_crossed(h):
        return pltpu.make_async_copy(r.crossed.at[:, rows(h)], r.crossed_out.at[:, rows(h)], r.out_sem.at[h])

    def pre(h):
        def part(t):
            return dot(side_by_side(r.crossed, h), r.weight[:, pl.ds(pl.multiple_of(t * width, width), width)])

        def other_core(y):
            r.sib_send[h, y] = part(y * 2 + 1 - core).astype(BF)
            to_sibling(h, y).start()

        def my_core(i):
            dy = lax.rem(i + 1, chips)
            y = lax.rem(chip + dy, chips)
            mine = part(y * 2 + core)
            to_sibling(h, y).wait_recv()
            mine = mine + r.sib_recv[h, y].astype(F32)

            @pl.when(dy == 0)
            def _():
                r.pre_own[h] = mine

            @pl.when(dy > 0)
            def _():
                r.pre_send[h, dy] = mine.astype(BF)
                pre_to(h, dy).start()

        each(chips, other_core)
        each(chips, my_core)

    def activate(h):
        value = r.pre_own[h] + r.hbias[:, pl.ds(pl.multiple_of(lane * width, width), width)]
        for dy in range(1, chips):
            pre_to(h, dy).wait_recv()
            value = value + r.pre_recv[h, dy].astype(F32)
        sig = jax.nn.sigmoid(value)
        r.hidden[rows(h), :] = (value * sig).astype(BF)
        r.gpre[h, lane] = (r.hgrad[rows(h), :].astype(F32) * sig * (1.0 + value * (1.0 - sig))).astype(BF)
        each(chips, lambda dy: gpre_to(h, dy).start(), 1)
        forward(h, 0).start()

    def pass_on(h):
        def one(dy):
            gpre_to(h, dy).wait_recv()
            forward(h, dy).start()

        each(chips, one, 1)

    def back_chips(h, steps):
        sides = []
        for dy in steps:
            forward(h, dy).wait_recv()
            y = lax.rem(chip + chips - dy, chips)
            wide = pl.ds(pl.multiple_of(y * 2 * width, 2 * width), 2 * width)
            sides.append((y, wide))

        def columns(n):
            here = pl.ds(pl.multiple_of(n * 512, 512), 512)
            added = None
            for y, wide in sides:
                grads = jnp.concatenate([r.gpre[h, y * 2], r.gpre[h, y * 2 + 1]], 1)
                term = dot(grads, r.weight[here, wide], ((1,), (1,)))
                added = term if added is None else added + term
            if 0 in steps:
                r.gcross[rows(h), here] = added
            else:
                r.gcross[rows(h), here] += added

        each(total // 512, columns)

    def rank_grad(h):
        for q in range(n_node):
            here = slice(q * 128, (q + 1) * 128)
            r.gx[q, rows(h), :] = (r.gcross[rows(h), here] * r.x[rows(h), here].astype(F32)).astype(BF)
        send_parts(1, h, lambda here: dot(side_by_side(r.gx, h), r.up[here, :], ((1,), (1,))))

    def input_grad(h):
        each(n_local, lambda d: share_to(1, h, d).wait_recv(), 1)

        def columns(n):
            here = pl.ds(pl.multiple_of(n * 512, 512), 512)
            grads = r.gcross[rows(h), here]
            result = grads * r.term[rows(h), here] + grads + dot(whole_rank(1, h), r.down[here, :], ((1,), (1,)))
            result = result.astype(BF)
            for i in range(4):
                r.gx[n * 4 + i, rows(h), :] = result[:, i * 128 : (i + 1) * 128]

        each(total // 512, columns)

    def pack_back(p):
        here = slice(p * small, (p + 1) * small)
        each(n_local, lambda d: out_lane(p, d).wait_send(), 1)

        def send(d):
            target = lax.rem(lane + d, n_local)
            for c in range(cap):
                r.packed[p, d, c] = r.gx[r.slots[2, target * cap + c], here]
            back_lane(p, d).start()

        each(n_local, send, 1)
        for c in range(cap):
            returned[p][lane * cap + c] = r.gx[r.slots[2, lane * cap + c], here]

    def route_piece(p):
        each(n_node, lambda k: out_node(p, k).wait_send(), 1)
        each(n_local, lambda d: back_lane(p, d).wait_recv(), 1)

        def send(k):
            r.pooled[p, k] = returned[p][r.slots[3, lax.rem(node + k, n_node)]]
            back_node(p, k).start()

        each(n_node, send, 1)
        r.home[p, node] = returned[p][r.slots[3, node]]

    def add_piece(p):
        each(n_node, lambda k: back_node(p, k).wait_recv(), 1)

        def one_chunk(c):
            t = p * chunks + c
            buffer = lax.rem(t, 2)
            for i in range(at_once * small // 128):
                parts = [
                    r.home[p, lax.rem(node + c * at_once + i * (128 // small) + j, n_node)] for j in range(128 // small)
                ]
                r.home_t[:, i * 128 : (i + 1) * 128] = jnp.concatenate(parts, 0).T
            fetch(t).wait()
            for n in range(r.sums.shape[1] // 512):
                here = slice(n * 512, (n + 1) * 512)
                r.sums[:, here] += dot(r.home_t[...], r.counts[buffer, :, here])

            @pl.when(t + 2 < PIECES * chunks)
            def _():
                fetch(t + 2).start()

        each(chunks, one_chunk)

    my_columns = pl.ds(pl.multiple_of(lane * width, width), width)
    loads = [
        pltpu.make_async_copy(r.down_hbm, r.down, r.load_sem.at[0]),
        pltpu.make_async_copy(r.up_hbm, r.gx, r.load_sem.at[1]),
        pltpu.make_async_copy(r.weight_hbm, r.weight, r.load_sem.at[2]),
        pltpu.make_async_copy(r.grad_hbm.at[:, my_columns], r.hgrad, r.load_sem.at[3]),
    ]
    barrier = greet(n_node, n_local, node, lane)
    fill = [
        pltpu.make_async_copy(r.idx_hbm, r.idx, r.load_sem.at[4]),
        pltpu.make_async_copy(r.size_hbm, r.size, r.load_sem.at[5]),
        pltpu.make_async_copy(r.table_hbm, r.table, r.load_sem.at[6]),
    ]
    for load in fill:
        load.start()
    r.slots_v[...] = jnp.zeros_like(r.slots_v)
    find_slots()
    for load in fill:
        load.wait()
    for load in loads:
        load.start()
    flatten_picks(r.idx, r.size, r.iota, r.key, r.low)
    each(chunks, lambda c: pool_chunk(0, c))
    pl.semaphore_wait(barrier, n_node + n_local - 2)
    for c in range(chunks):
        send_chunk(0, c)

    def turn(p):
        def one_chunk(c):
            pool_chunk(p, c)
            for piece in range(1, PIECES):

                @pl.when(p == piece)
                def _():
                    send_chunk(piece, c)

        each(chunks, one_chunk)
        for piece in range(PIECES - LAG):

            @pl.when(p == piece + LAG)
            def _():
                pack_piece(piece)

    each(PIECES, turn, 1)
    r.sums[...] = jnp.zeros_like(r.sums)
    for t in range(2):
        save(PIECES * chunks - 2 + t).wait()
    for t in range(2):
        fetch(t).start()
    for load in loads:
        load.wait()
    unpack_piece(0)
    unpack_piece(1)
    unpack_piece(3)
    unpack_piece(2)
    low_parts(0)
    pack_piece(6)
    unpack_piece(5)
    unpack_piece(4)
    lay_up()
    reduce_parts(0, 0)
    pack_piece(7)
    unpack_piece(6)
    cross(0)
    pre(0)
    unpack_piece(7)
    low_parts(1)
    activate(0)
    back_chips(0, [0])
    pass_on(0)
    reduce_parts(0, 1)
    back_chips(0, [1, 2, 3])
    rank_grad(0)
    cross(1)
    pre(1)
    reduce_parts(1, 0)
    activate(1)
    back_chips(1, [0])
    input_grad(0)
    pack_back(0)
    pack_back(1)
    pass_on(1)
    back_chips(1, [1, 2, 3])
    rank_grad(1)
    route_piece(0)
    pack_back(2)
    reduce_parts(1, 1)
    pack_back(3)
    route_piece(1)
    input_grad(1)
    pack_back(4)
    pack_back(5)
    route_piece(2)
    add_piece(0)
    route_piece(3)
    pack_back(6)
    add_piece(1)
    pack_back(7)
    route_piece(4)
    add_piece(2)
    add_piece(3)
    route_piece(5)
    add_piece(4)
    route_piece(6)
    route_piece(7)
    add_piece(5)
    add_piece(6)
    add_piece(7)
    for n in range(r.sums.shape[1] // 128):
        r.table_grad[n * 128 : (n + 1) * 128, :] = r.sums[:, n * 128 : (n + 1) * 128].T

    for p in range(PIECES):
        each(n_node, lambda k: back_node(p, k).wait_send(), 1)
        each(n_local, lambda d: back_lane(p, d).wait_send(), 1)
    for h in range(HALVES):
        keep_crossed(h).wait()
        for w in range(2):
            each(n_local, lambda d: part_to(w, h, d).wait_send(), 1)
            each(n_local, lambda d: share_to(w, h, d).wait_send(), 1)
        each(chips, lambda y: to_sibling(h, y).wait_send())
        each(chips, lambda dy: pre_to(h, dy).wait_send(), 1)
        each(chips, lambda dy: gpre_to(h, dy).wait_send(), 1)
        each(chips, lambda dy: forward(h, dy).wait_send())


VMEM = pl.BlockSpec(memory_space=pltpu.VMEM)
ANY = pl.BlockSpec(memory_space=pl.ANY)
SEM = pltpu.SemaphoreType.DMA


def train_step(operands, features, samples, n_node, n_local, cap):
    depth, hidden = operands["down_hbm"].shape[1], operands["weight_hbm"].shape[1]
    total = operands["down_hbm"].shape[0]
    table_rows, emb = operands["table_hbm"].shape
    groups = operands["idx_hbm"].shape[1] // BAG_GROUP
    small, half, width, chips = samples // PIECES, samples // HALVES, hidden // n_local, n_local // 2
    kept = (groups // CHUNK, CHUNK * BAG_GROUP, table_rows)
    outs = {
        "crossed_out": (jax.ShapeDtypeStruct((features, samples, emb), BF), ANY),
        "hidden": (jax.ShapeDtypeStruct((samples, width), BF), VMEM),
        "table_grad": (jax.ShapeDtypeStruct((table_rows, emb), F32), VMEM),
        "kept": (jax.ShapeDtypeStruct(kept, BF), ANY),
    }
    parts = pltpu.VMEM((2, HALVES, n_local, half // n_local, depth), BF)
    quarter = pltpu.VMEM((HALVES, chips, half, width), BF)
    scratch = {
        "idx": pltpu.VMEM(operands["idx_hbm"].shape, jnp.int32),
        "size": pltpu.VMEM(operands["size_hbm"].shape, jnp.int32),
        "table": pltpu.VMEM((table_rows, emb), BF),
        "slots_v": pltpu.VMEM((8, operands["owner"].shape[1]), jnp.int32),
        "slots": pltpu.SMEM((8, operands["owner"].shape[1]), jnp.int32),
        "iota": pltpu.VMEM((LOW, LOW), BF),
        "key": pltpu.VMEM((groups, LOW), F32),
        "low": pltpu.VMEM((groups, LOW), F32),
        "counts": pltpu.VMEM((2, *kept[1:]), BF),
        "pooled": pltpu.VMEM((PIECES, n_node, small, emb), BF),
        "packed": pltpu.VMEM((PIECES, n_local, cap, small, emb), BF),
        "home": pltpu.VMEM((PIECES, n_node, small, emb), BF),
        "home_t": pltpu.VMEM((emb, kept[1]), BF),
        "sums": pltpu.VMEM((emb, table_rows), F32),
        "x": pltpu.VMEM((samples, total), BF),
        "down": pltpu.VMEM((total, depth), BF),
        "up": pltpu.VMEM((depth, total), BF),
        "weight": pltpu.VMEM((total, hidden), BF),
        "hgrad": pltpu.VMEM((samples, width), BF),
        "term": pltpu.VMEM((samples, total), F32),
        "gcross": pltpu.VMEM((samples, total), F32),
        "gx": pltpu.VMEM((features, samples, emb), BF),
        "crossed": pltpu.VMEM((features, samples, emb), BF),
        "out_sem": SEM((HALVES,)),
        "rank_send": parts,
        "rank_recv": parts,
        "rank": parts,
        "sib_send": quarter,
        "sib_recv": quarter,
        "pre_send": quarter,
        "pre_recv": quarter,
        "pre_own": pltpu.VMEM((HALVES, half, width), F32),
        "gpre": pltpu.VMEM((HALVES, n_local, half, width), BF),
        "load_sem": SEM((8,)),
        "save_sem": SEM((2,)),
        "fetch_sem": SEM((2,)),
    }
    for p in range(PIECES):
        scratch[f"arrived{p}"] = pltpu.VMEM((n_node, small, emb), BF)
        scratch[f"landed{p}"] = pltpu.VMEM((n_local * cap, small, emb), BF)
        scratch[f"returned{p}"] = pltpu.VMEM((n_local * cap, small, emb), BF)
    for names, shape in (
        (("on", "bn"), (PIECES, n_node)),
        (("ol", "bl"), (PIECES, n_local)),
        (("rk", "sh"), (2, HALVES, n_local)),
        (("sb", "pr", "gp", "fw"), (HALVES, chips)),
    ):
        for name in names:
            scratch[name + "_s"] = SEM(shape)
            scratch[name + "_r"] = SEM(shape)
    specs = [ANY if name.endswith("_hbm") else VMEM for name in operands]
    names = [*operands, *outs, *scratch]
    return pl.pallas_call(
        functools.partial(step_kernel, names, n_node, n_local),
        out_shape=[shape for shape, _ in outs.values()],
        in_specs=specs,
        out_specs=[spec for _, spec in outs.values()],
        scratch_shapes=list(scratch.values()),
        compiler_params=pltpu.CompilerParams(collective_id=0, has_side_effects=True, vmem_limit_bytes=VMEM_LIMIT),
        name="train_step",
    )(*operands.values())


def hand_out_kernel(count, *refs):
    given, taken, held = refs[:count], refs[count : 2 * count], refs[2 * count : 3 * count]
    read_sem, write_sem = refs[3 * count :]
    reads, writes = [], []
    for source, target, middle in zip(given, taken, held):
        rows = source.shape[0] // 4
        for i in range(4):
            part, at = pl.ds(i * rows, rows), len(reads)
            reads.append(pltpu.make_async_copy(source.at[part], middle.at[part], read_sem.at[at]))
            writes.append(pltpu.make_async_copy(middle.at[part], target.at[part], write_sem.at[at]))
    for copy in reads:
        copy.start()
    for read, write in zip(reads, writes):
        read.wait()
        write.start()
    for copy in writes:
        copy.wait()


def hand_out(*arrays):
    count = len(arrays)
    return pl.pallas_call(
        functools.partial(hand_out_kernel, count),
        out_shape=[jax.ShapeDtypeStruct(a.shape, a.dtype) for a in arrays],
        in_specs=[ANY] * count,
        out_specs=[ANY] * count,
        scratch_shapes=[*[pltpu.VMEM(a.shape, a.dtype) for a in arrays], SEM((4 * count,)), SEM((4 * count,))],
        compiler_params=pltpu.CompilerParams(vmem_limit_bytes=VMEM_LIMIT),
        name="hand_out",
    )(*arrays)


def on_device(
    owner_map,
    bag_sizes,
    indices,
    tables,
    cross_down,
    cross_up,
    cross_bias,
    mlp_weight,
    mlp_bias,
    hidden_grad,
):
    node_count = lax.axis_size("node")
    lane_count = lax.axis_size("local")
    capacity = node_count // lane_count + 1
    samples = hidden_grad.shape[0]
    hidden_width = hidden_grad.shape[1]
    operands = {
        "owner": owner_map.reshape(1, -1),
        "bias": cross_bias.reshape(1, -1),
        "hbias": mlp_bias.reshape(1, -1),
        "idx_hbm": indices[0].T,
        "size_hbm": bag_sizes,
        "table_hbm": tables,
        "grad_hbm": hidden_grad,
        "down_hbm": cross_down.reshape(-1, cross_down.shape[2]),
        "up_hbm": cross_up.reshape(node_count, -1, cross_up.shape[2]),
        "weight_hbm": mlp_weight.reshape(-1, hidden_width),
    }
    crossed, hidden, table_grad, _ = train_step(operands, node_count, samples, node_count, lane_count, capacity)
    return hand_out(crossed, hidden, table_grad)


def solution(mesh):
    return jax.shard_map(
        on_device,
        mesh=mesh,
        in_specs=(
            P(),
            P(("node", "local"), None),
            P(("node", "local"), None, None),
            P(("node", "local"), None),
            P("local", None, None),
            P(None, "local", None),
            P("local", None),
            P("local", None, None),
            P(),
            P("node", None),
        ),
        out_specs=(P("local", "node", None), P("node", "local"), P(("node", "local"), None)),
        check_vma=False,
    )
```
